128 devices in a mesh: row: 16 (over z, y_hi, core), col: 8 (over x, y_lo).
Axes of the slice: x: 4, y: 4 (y_hi: 2, y_lo: 2; y = y_hi * 2 + y_lo), z: 4, core: 2. Of those that a mesh axis runs over, the one named last changes fastest.
Arguments:
- inverse_tiles: bfloat16 [24576, 24576], P('row', 'col'), may hold values from -6 to 6
- factor: bfloat16 [24576, 2048], P('row', 'col'), may hold values from -0.0390625 to 0.0390625
- block_mask: int32 [192, 16], replicated, may hold values 0 or 1
- diag_inverse: float32 [16, 128, 128], replicated, may hold values from -6 to 6
Outputs:
- off_block: bfloat16 [2048, 24576], P('col', 'row')
- diag_block: float32 [16, 128, 128], P('col')
The draws below stay inside these ranges and needn't reach their ends.
All inputs are finite; a program needn't handle non-finite values.
Results may differ from the reference program's by a relative error of at most 0.012.
Values may be sent and summed in bfloat16 or wider, within the bound.
A program may use at most 128 MiB of HBM per device.

```python
import jax
import jax.numpy as jnp
from jax import lax

W = 128
NSUP = 16
R = 24576
NB = 192


def plant(array, key, least, top_value):
    place = [jax.random.randint(jax.random.fold_in(key, axis), (), 0, length) for axis, length in enumerate(array.shape)]
    widest = array.shape.index(max(array.shape))
    neighbour = place[:widest] + [(place[widest] + 1) % array.shape[widest]] + place[widest + 1:]
    return array.at[tuple(place)].set(least).at[tuple(neighbour)].set(top_value)


def shard_levels(stream_key, extent, shards, low, top_value):
    factor_of, own = 1.0, jax.random.fold_in(stream_key, 6)
    for position, shards_of in shards:
        steps = jnp.exp(jax.random.uniform(jax.random.fold_in(own, position), (shards_of,), jnp.float32, low / len(shards), top_value / len(shards)))
        factor_of = factor_of * jnp.repeat(steps, extent[position] // shards_of).reshape([-1 if axis == position else 1 for axis in range(len(extent))])
    return factor_of


def scatter_about(key, dims, deviation, limit, pieces=(), kind=jnp.bfloat16):
    level = shard_levels(key, dims, pieces, -0.22, 0.18) if pieces else 1.0
    drawn = jax.random.normal(key, dims, jnp.float32) * deviation * level
    return jnp.minimum(jnp.maximum(drawn, -limit), limit).astype(kind)


def setup_inputs(seed: int = 0) -> dict:
    key_of = jax.random.split(jax.random.key(seed), 5)
    inverse_tiles = scatter_about(key_of[0], (R, R), 1.0, 6.0, ((0, 16), (1, 8)))
    factor = scatter_about(key_of[1], (R, NSUP * W), R ** -0.5, 0.0390625, ((0, 16), (1, 8)))
    block_mask = plant((jax.random.randint(key_of[2], (NB, NSUP), 0, 5) < 4).astype(jnp.int32), jax.random.fold_in(key_of[2], 1), 0, 1)
    diag_inverse = scatter_about(key_of[3], (NSUP, W, W), 1.0, 6.0, (), jnp.float32)
    return {"inverse_tiles": inverse_tiles, "factor": factor, "block_mask": block_mask, "diag_inverse": diag_inverse}


def reference(inverse_tiles, factor, block_mask, diag_inverse):
    keep_mask = jnp.repeat(jnp.repeat(block_mask, W, 0), W, 1).astype(jnp.bfloat16)
    masked = factor * keep_mask
    product = jnp.dot(inverse_tiles, masked, preferred_element_type=jnp.float32)
    off_block = (-product).T.astype(jnp.bfloat16)
    left_factor = masked.astype(jnp.float32).reshape(-1, NSUP, W)
    right_product = product.reshape(-1, NSUP, W)
    diag_block = diag_inverse + jnp.einsum("rja,rjb->jab", left_factor, right_product, precision=lax.Precision.HIGHEST)
    return off_block, diag_block
```

```python
import jax
import jax.numpy as jnp
from jax import lax
from jax.experimental import pallas as pl
from jax.experimental.pallas import tpu as pltpu
from jax.sharding import PartitionSpec as P

MESH = pl.DeviceIdType.MESH
BF = jnp.bfloat16
F32 = jnp.float32
W = 128
SLOTS = 2
PARTS = 3
STEPS = SLOTS * PARTS

T, Y, ZRO, ZLO, ZRP, ZLP, RR, RL = range(8)
SIB = 8
GATHER = 16
QR, QL, FR0, FR1, FL0, FL1, YL = range(7)
REDUCE = 7


def kernel(
    fac, a_hbm, mask, dinv_hbm, off, diag,
    a, dinv, masked, x, part, own, relay, fin, ysend, yrecv, dacc, dsend, drecv, dsum, dall,
    local_sem, g_send, g_recv, r_send, r_recv, d_send, d_recv,
):
    rows = fac.shape[0]
    slice_rows = rows // PARTS
    row, col = lax.axis_index("row"), lax.axis_index("col")
    z, yh, p = row // 4, (row // 2) % 2, row % 2
    xi, yl = col // 2, col % 2
    zr, zl, z2 = (z + 1) % 4, (z + 3) % 4, (z + 2) % 4
    xr, xl, x2 = (xi + 1) % 4, (xi + 3) % 4, (xi + 2) % 4

    def dev(z_, yh_, p_, x_, yl_):
        return (z_ * 4 + yh_ * 2 + p_, x_ * 2 + yl_)

    turned = dev(xi, yl, p, z, yh)
    at_home = jnp.logical_and(xi == z, yl == yh)
    partner = dev(z, 1 - yh, p, xi, yl)
    z_right, z_left = dev(zr, yh, p, xi, yl), dev(zl, yh, p, xi, yl)
    sibling = dev(z, yh, 1 - p, xi, yl)
    x_right, x_left = dev(z, yh, p, xr, yl), dev(z, yh, p, xl, yl)
    y_near = dev(z, yh, p, xi, 1 - yl)

    a_copy = pltpu.make_async_copy(a_hbm, a, local_sem.at[0])
    a_copy.start()
    dinv_copy = pltpu.make_async_copy(dinv_hbm.at[pl.ds(col * 16, 16)], dinv, local_sem.at[1])
    dinv_copy.start()

    barrier = pltpu.get_barrier_semaphore()

    @pl.loop(1, 16)
    def _(o):
        pl.semaphore_signal(barrier, inc=1, device_id=((row + o) % 16, col), device_id_type=MESH)

    for d in (x_right, x_left, y_near):
        pl.semaphore_signal(barrier, inc=1, device_id=d, device_id_type=MESH)

    @pl.when(jnp.logical_not(at_home))
    def _():
        pl.semaphore_signal(barrier, inc=1, device_id=turned, device_id_type=MESH)

    for s in range(SLOTS):
        for b in range(rows // W):
            keep = mask[row * (rows // W) + b, col * SLOTS + s].astype(F32)
            block = fac[b * W : (b + 1) * W, s * W : (s + 1) * W].astype(F32)
            masked[s, b * W : (b + 1) * W, :] = (block * keep).astype(BF)

    pl.semaphore_wait(barrier, jnp.where(at_home, 18, 19))

    pending = []

    def remote(src, dst, send, recv, i, device):
        return pltpu.make_async_remote_copy(
            src_ref=src, dst_ref=dst, send_sem=send.at[i], recv_sem=recv.at[i],
            device_id=device, device_id_type=MESH,
        )

    k, kp = 2 * z + yh, 2 * z + 1 - yh
    lo, lp = 2 * zl + yh, 2 * zl + 1 - yh
    ro, rp = 2 * zr + yh, 2 * zr + 1 - yh
    fo, fp = 2 * z2 + yh, 2 * z2 + 1 - yh

    gcopies = {}

    def gather_copy(s, i, g, device):
        c = remote(x.at[s, p, g], x.at[s, p, g], g_send, g_recv, s * GATHER + i, device)
        gcopies[s, i] = c
        return c

    def start_gather(s, i, g, device):
        c = gather_copy(s, i, g, device)
        c.start()
        pending.append(c)

    def got(s, i):
        gcopies[s, i].wait_recv()

    def turn_copies(s):
        away = remote(masked.at[s], x.at[s, p, 2 * xi + yl], g_send, g_recv, s * GATHER + T, turned)
        here = pltpu.make_async_copy(masked.at[s], x.at[s, p, k], g_recv.at[s * GATHER + T])
        return away, here

    def start_turn(s):
        away, here = turn_copies(s)

        @pl.when(jnp.logical_not(at_home))
        def _():
            away.start()

        @pl.when(at_home)
        def _():
            here.start()

    def event0(s):
        away, here = turn_copies(s)

        @pl.when(jnp.logical_not(at_home))
        def _():
            away.wait_recv()
            away.wait_send()

        @pl.when(at_home)
        def _():
            here.wait()

        start_gather(s, ZRO, k, z_right)
        start_gather(s, ZLO, k, z_left)
        start_gather(s, Y, k, partner)
        start_gather(s, SIB + 0, k, sibling)

    def event1(s):
        got(s, Y)
        start_gather(s, ZRP, kp, z_right)
        start_gather(s, ZLP, kp, z_left)
        start_gather(s, SIB + 1, kp, sibling)

    def event2(s):
        got(s, ZRO)
        start_gather(s, RR, lo, z_right)
        start_gather(s, SIB + 2, lo, sibling)
        got(s, ZLO)
        start_gather(s, SIB + 3, ro, sibling)

    def event3(s):
        got(s, ZLP)
        start_gather(s, RL, rp, z_left)
        start_gather(s, SIB + 4, rp, sibling)
        got(s, ZRP)
        start_gather(s, SIB + 5, lp, sibling)

    def event4(s):
        got(s, RR)
        start_gather(s, SIB + 6, fo, sibling)
        got(s, RL)
        start_gather(s, SIB + 7, fp, sibling)

    def event5(s):
        for i in range(8):
            got(s, SIB + i)

    def product(t, dest):
        s, m = divmod(t, PARTS)
        here = slice(m * slice_rows, (m + 1) * slice_rows)
        total = None
        for half in range(2):
            right = jnp.concatenate([x[s, half, 2 * dest], x[s, half, 2 * dest + 1]], axis=1)
            term = jnp.dot(a[here, half * rows : (half + 1) * rows], right, preferred_element_type=F32)
            total = term if total is None else total + term
        return total

    rcopies = {}

    def start_reduce(t, i, src, dst, device):
        c = remote(src, dst, r_send, r_recv, t * REDUCE + i, device)
        c.start()
        rcopies[t, i] = c
        pending.append(c)

    def arrived(t, i):
        rcopies[t, i].wait_recv()

    def multiply(t):
        @pl.loop(0, 3)
        def _(j):
            block = product(t, (xi + 1 + j) % 4)
            part[t, j, 0] = block[:, :W].astype(BF)
            part[t, j, 1] = block[:, W:].astype(BF)

        start_reduce(t, QR, part.at[t, 1, 0], relay.at[t, 0], x_right)
        start_reduce(t, QL, part.at[t, 1, 1], relay.at[t, 1], x_left)
        start_reduce(t, FR1, part.at[t, 0, 1], fin.at[t, 0, 1], x_right)
        start_reduce(t, FL0, part.at[t, 2, 0], fin.at[t, 1, 0], x_left)
        block = product(t, xi)
        own[t, 0] = block[:, :W]
        own[t, 1] = block[:, W:]

    def pass_on(t):
        arrived(t, QR)
        part[t, 0, 0] = (part[t, 0, 0].astype(F32) + relay[t, 0].astype(F32)).astype(BF)
        start_reduce(t, FR0, part.at[t, 0, 0], fin.at[t, 0, 0], x_right)
        arrived(t, QL)
        part[t, 2, 1] = (part[t, 2, 1].astype(F32) + relay[t, 1].astype(F32)).astype(BF)
        start_reduce(t, FL1, part.at[t, 2, 1], fin.at[t, 1, 1], x_left)

    def finish(t):
        for i in (FR0, FR1, FL0, FL1):
            arrived(t, i)
        far = 1 - yl
        ysend[t] = (own[t, far] + fin[t, 0, far].astype(F32) + fin[t, 1, far].astype(F32)).astype(BF)
        start_reduce(t, YL, ysend.at[t], yrecv.at[t], y_near)
        own[t, yl] = own[t, yl] + fin[t, 0, yl].astype(F32) + fin[t, 1, yl].astype(F32)

    def put(t):
        s, m = divmod(t, PARTS)
        here = slice(m * slice_rows, (m + 1) * slice_rows)
        arrived(t, YL)
        turned_product = (own[t, yl] + yrecv[t].astype(F32)).T
        off[s * W : (s + 1) * W, here] = (-turned_product).astype(BF)
        high = turned_product.astype(BF)
        low = (turned_product - high.astype(F32)).astype(BF)
        right = masked[s, here, :]
        term = jnp.dot(high, right, preferred_element_type=F32) + jnp.dot(
            low, right, preferred_element_type=F32
        )
        if m == 0:
            dacc[s] = term
        else:
            dacc[s] += term

    start_turn(0)
    start_turn(1)
    event0(0)
    event1(0)
    event2(0)
    event3(0)
    event0(1)
    event4(0)
    event1(1)
    a_copy.wait()
    dinv_copy.wait()
    event5(0)
    multiply(0)
    event2(1)
    multiply(1)
    pass_on(0)
    event3(1)
    multiply(2)
    pass_on(1)
    finish(0)
    event4(1)
    pass_on(2)
    finish(1)
    put(0)
    event5(1)
    multiply(3)
    finish(2)
    put(1)
    multiply(4)
    pass_on(3)
    put(2)
    multiply(5)
    pass_on(4)
    finish(3)
    pass_on(5)
    finish(4)
    put(3)
    finish(5)
    put(4)
    put(5)

    for s in range(SLOTS):
        dsend[s * 8 : (s + 1) * 8] = dacc[s].T.reshape(8, 16, W)

    def scatter_copy(o):
        to = (row + o) % 16
        return remote(dsend.at[to], drecv.at[o], d_send, d_recv, o, (to, col))

    def spread_copy(o):
        to = (row + o) % 16
        return remote(dsum, dall.at[row], d_send, d_recv, 16 + o, (to, col))

    @pl.loop(1, 16)
    def _(o):
        scatter_copy(o).start()

    @pl.loop(1, 16)
    def _(o):
        scatter_copy(o).wait_recv()

    total = dsend[row] + dinv[row]
    for o in range(1, 16):
        total = total + drecv[o]
    dsum[...] = total

    @pl.loop(1, 16)
    def _(o):
        spread_copy(o).start()

    diag[row] = total

    @pl.loop(1, 16)
    def _(o):
        spread_copy(o).wait_recv()
        since = (row + 16 - o) % 16
        diag[since] = dall[since]

    @pl.loop(1, 16)
    def _(o):
        scatter_copy(o).wait_send()
        spread_copy(o).wait_send()

    for c in pending:
        c.wait_send()


def per_device(inverse_tiles, factor, block_mask, diag_inverse):
    rows, depth = inverse_tiles.shape
    cols = factor.shape[1]
    part_rows = rows // PARTS
    vmem = pl.BlockSpec(memory_space=pltpu.VMEM)
    anywhere = pl.BlockSpec(memory_space=pl.ANY)
    off, diag = pl.pallas_call(
        kernel,
        out_shape=(
            jax.ShapeDtypeStruct((cols, rows), BF),
            jax.ShapeDtypeStruct((16, 16, W), F32),
        ),
        in_specs=[vmem, anywhere, pl.BlockSpec(memory_space=pltpu.SMEM), anywhere],
        out_specs=(vmem, vmem),
        scratch_shapes=[
            pltpu.VMEM((rows, depth), BF),
            pltpu.VMEM((16, 16, W), F32),
            pltpu.VMEM((SLOTS, rows, W), BF),
            pltpu.VMEM((SLOTS, 2, 8, rows, W), BF),
            pltpu.VMEM((STEPS, 3, 2, part_rows, W), BF),
            pltpu.VMEM((STEPS, 2, part_rows, W), F32),
            pltpu.VMEM((STEPS, 2, part_rows, W), BF),
            pltpu.VMEM((STEPS, 2, 2, part_rows, W), BF),
            pltpu.VMEM((STEPS, part_rows, W), BF),
            pltpu.VMEM((STEPS, part_rows, W), BF),
            pltpu.VMEM((SLOTS, W, W), F32),
            pltpu.VMEM((16, 16, W), F32),
            pltpu.VMEM((16, 16, W), F32),
            pltpu.VMEM((16, W), F32),
            pltpu.VMEM((16, 16, W), F32),
            pltpu.SemaphoreType.DMA((2,)),
            pltpu.SemaphoreType.DMA((SLOTS * GATHER,)),
            pltpu.SemaphoreType.DMA((SLOTS * GATHER,)),
            pltpu.SemaphoreType.DMA((STEPS * REDUCE,)),
            pltpu.SemaphoreType.DMA((STEPS * REDUCE,)),
            pltpu.SemaphoreType.DMA((32,)),
            pltpu.SemaphoreType.DMA((32,)),
        ],
        compiler_params=pltpu.CompilerParams(
            collective_id=0, has_side_effects=True, vmem_limit_bytes=58 * 1024 * 1024
        ),
    )(factor, inverse_tiles, block_mask, diag_inverse.reshape(8 * 16, 16, W))
    return off, diag.reshape(2, W, W)


def solution(mesh):
    return jax.shard_map(
        per_device,
        mesh=mesh,
        in_specs=(P("row", "col"), P("row", "col"), P(), P()),
        out_specs=(P("col", "row"), P("col", None, None)),
        check_vma=False,
    )
```

```python
import jax
import jax.numpy as jnp
from jax import lax
from jax.experimental import pallas as pl
from jax.experimental.pallas import tpu as pltpu
from jax.sharding import PartitionSpec as P

MESH = pl.DeviceIdType.MESH
BF = jnp.bfloat16
F32 = jnp.float32
W = 128
SLOTS = 2
PARTS = 3
STEPS = SLOTS * PARTS

YA, YB, ZRO, ZLO, ZRP, ZLP, RR, RL = range(8)
SIB = 8
GATHER = 16
QR, QL, FR0, FR1, FL0, FL1, YL = range(7)
REDUCE = 7


def kernel(
    fac, a_hbm, mask, dinv_hbm, off, diag,
    a, dinv, masked, x, hub, turned, part, own, relay, fin, ysend, yrecv, dacc, dsend, drecv, dsum, dall,
    local_sem, g_send, g_recv, h_send, h_recv, f_send, t_recv, r_send, r_recv, d_send, d_recv,
):
    rows = fac.shape[0]
    slice_rows = rows // PARTS
    row, col = lax.axis_index("row"), lax.axis_index("col")
    z, yh, p = row // 4, (row // 2) % 2, row % 2
    xi, yl = col // 2, col % 2
    zr, zl, z2 = (z + 1) % 4, (z + 3) % 4, (z + 2) % 4
    xr, xl, x2 = (xi + 1) % 4, (xi + 3) % 4, (xi + 2) % 4

    def dev(z_, yh_, p_, x_, yl_):
        return (z_ * 4 + yh_ * 2 + p_, x_ * 2 + yl_)

    on_diagonal = xi == z
    moves_near = yl != yh
    y_first, y_second = dev(z, yl, p, xi, yh), dev(z, 1 - yl, p, xi, yh)
    z_right, z_left = dev(zr, yh, p, xi, yl), dev(zl, yh, p, xi, yl)
    sibling = dev(z, yh, 1 - p, xi, yl)
    x_right, x_left = dev(z, yh, p, xr, yl), dev(z, yh, p, xl, yl)
    y_near = dev(z, yh, p, xi, 1 - yl)

    a_copy = pltpu.make_async_copy(a_hbm, a, local_sem.at[0])
    a_copy.start()
    dinv_copy = pltpu.make_async_copy(dinv_hbm.at[pl.ds(col * 16, 16)], dinv, local_sem.at[1])
    dinv_copy.start()

    barrier = pltpu.get_barrier_semaphore()

    @pl.loop(1, 16)
    def _(o):
        pl.semaphore_signal(barrier, inc=1, device_id=((row + o) % 16, col), device_id_type=MESH)

    for d in (x_right, x_left, dev(z, yh, p, x2, yl), y_near):
        pl.semaphore_signal(barrier, inc=1, device_id=d, device_id_type=MESH)

    @pl.when(moves_near)
    def _():
        pl.semaphore_signal(barrier, inc=1, device_id=y_first, device_id_type=MESH)

    for s in range(SLOTS):
        for b in range(rows // W):
            keep = mask[row * (rows // W) + b, col * SLOTS + s].astype(F32)
            block = fac[b * W : (b + 1) * W, s * W : (s + 1) * W].astype(F32)
            masked[s, b * W : (b + 1) * W, :] = (block * keep).astype(BF)

    pl.semaphore_wait(barrier, jnp.where(moves_near, 20, 19))

    pending = []

    def remote(src, dst, send, recv, i, device):
        return pltpu.make_async_remote_copy(
            src_ref=src, dst_ref=dst, send_sem=send.at[i], recv_sem=recv.at[i],
            device_id=device, device_id_type=MESH,
        )

    k, kp = 2 * z + yh, 2 * z + 1 - yh
    lo, lp = 2 * zl + yh, 2 * zl + 1 - yh
    ro, rp = 2 * zr + yh, 2 * zr + 1 - yh
    fo, fp = 2 * z2 + yh, 2 * z2 + 1 - yh

    gcopies = {}

    def gather_copy(s, i, g, device):
        c = remote(x.at[s, p, g], x.at[s, p, g], g_send, g_recv, s * GATHER + i, device)
        gcopies[s, i] = c
        return c

    def start_gather(s, i, g, device):
        c = gather_copy(s, i, g, device)
        c.start()
        pending.append(c)

    def got(s, i):
        gcopies[s, i].wait_recv()

    halves = (slice(0, rows // 2), slice(rows // 2, rows))

    def to_hub(s, h):
        j = (xi - z + 4) % 4 if h == 0 else (z - xi + 4) % 4
        device = dev(z, yh, p, z, yl) if h == 0 else dev(xi, yh, p, xi, yl)
        i = (s * 2 + h) * 4
        return pltpu.make_async_remote_copy(
            src_ref=masked.at[s, halves[h]], dst_ref=hub.at[s, h, j],
            send_sem=h_send.at[s * 2 + h], recv_sem=h_recv.at[i + j],
            device_id=device, device_id_type=MESH,
        )

    def from_hub(s, h, j):
        device = dev((z + j) % 4, yh, p, xi, yl) if h == 0 else dev(z, yh, p, (xi + j) % 4, yl)
        i = (s * 2 + h) * 4
        return pltpu.make_async_remote_copy(
            src_ref=hub.at[s, h, j], dst_ref=turned.at[s, halves[h]],
            send_sem=f_send.at[i + j], recv_sem=t_recv.at[s * 2 + h],
            device_id=device, device_id_type=MESH,
        )

    def at_hub(s, h, j):
        i = (s * 2 + h) * 4
        return pltpu.make_async_copy(masked.at[s, halves[h]], hub.at[s, h, j], h_recv.at[i + j])

    def stay(s, h):
        return pltpu.make_async_copy(masked.at[s, halves[h]], turned.at[s, halves[h]], t_recv.at[s * 2 + h])

    def start_turn(s):
        for h in range(2):
            @pl.when(jnp.logical_not(on_diagonal))
            def _():
                to_hub(s, h).start()

            @pl.when(on_diagonal)
            def _():
                stay(s, h).start()

    def pass_hub(s):
        @pl.when(on_diagonal)
        def _():
            for j in (1, 3, 2):
                for h in range(2):
                    at_hub(s, h, j).wait()
                    from_hub(s, h, j).start()

    def end_turn(s):
        for h in range(2):
            stay(s, h).wait()

    def end_hub():
        for s in range(SLOTS):
            for h in range(2):
                @pl.when(jnp.logical_not(on_diagonal))
                def _():
                    to_hub(s, h).wait_send()

                @pl.when(on_diagonal)
                def _():
                    for j in (1, 3, 2):
                        from_hub(s, h, j).wait_send()

    def near_copies(s):
        away = remote(turned.at[s], x.at[s, p, 2 * z + yl], g_send, g_recv, s * GATHER + YA, y_first)
        here = pltpu.make_async_copy(turned.at[s], x.at[s, p, k], g_recv.at[s * GATHER + YA])
        return away, here

    def event0(s):
        end_turn(s)
        away, here = near_copies(s)

        @pl.when(moves_near)
        def _():
            away.start()

        @pl.when(jnp.logical_not(moves_near))
        def _():
            here.start()

        c = remote(turned.at[s], x.at[s, p, 2 * z + yl], g_send, g_recv, s * GATHER + YB, y_second)
        c.start()
        gcopies[s, YB] = c
        pending.append(c)
        here.wait()
        start_gather(s, ZRO, k, z_right)
        start_gather(s, ZLO, k, z_left)
        start_gather(s, SIB + 0, k, sibling)

    def event1(s):
        got(s, YB)
        start_gather(s, ZRP, kp, z_right)
        start_gather(s, ZLP, kp, z_left)
        start_gather(s, SIB + 1, kp, sibling)

    def event2(s):
        got(s, ZRO)
        start_gather(s, RR, lo, z_right)
        start_gather(s, SIB + 2, lo, sibling)
        got(s, ZLO)
        start_gather(s, SIB + 3, ro, sibling)

    def event3(s):
        got(s, ZLP)
        start_gather(s, RL, rp, z_left)
        start_gather(s, SIB + 4, rp, sibling)
        got(s, ZRP)
        start_gather(s, SIB + 5, lp, sibling)

    def event4(s):
        got(s, RR)
        start_gather(s, SIB + 6, fo, sibling)
        got(s, RL)
        start_gather(s, SIB + 7, fp, sibling)

    def event5(s):
        for i in range(8):
            got(s, SIB + i)

    def product(t, dest):
        s, m = divmod(t, PARTS)
        here = slice(m * slice_rows, (m + 1) * slice_rows)
        total = None
        for half in range(2):
            right = jnp.concatenate([x[s, half, 2 * dest], x[s, half, 2 * dest + 1]], axis=1)
            term = jnp.dot(a[here, half * rows : (half + 1) * rows], right, preferred_element_type=F32)
            total = term if total is None else total + term
        return total

    rcopies = {}

    def start_reduce(t, i, src, dst, device):
        c = remote(src, dst, r_send, r_recv, t * REDUCE + i, device)
        c.start()
        rcopies[t, i] = c
        pending.append(c)

    def arrived(t, i):
        rcopies[t, i].wait_recv()

    def multiply(t):
        @pl.loop(0, 3)
        def _(j):
            block = product(t, (xi + 1 + j) % 4)
            part[t, j, 0] = block[:, :W].astype(BF)
            part[t, j, 1] = block[:, W:].astype(BF)

        start_reduce(t, QR, part.at[t, 1, 0], relay.at[t, 0], x_right)
        start_reduce(t, QL, part.at[t, 1, 1], relay.at[t, 1], x_left)
        start_reduce(t, FR1, part.at[t, 0, 1], fin.at[t, 0, 1], x_right)
        start_reduce(t, FL0, part.at[t, 2, 0], fin.at[t, 1, 0], x_left)
        block = product(t, xi)
        own[t, 0] = block[:, :W]
        own[t, 1] = block[:, W:]

    def pass_on(t):
        arrived(t, QR)
        part[t, 0, 0] = (part[t, 0, 0].astype(F32) + relay[t, 0].astype(F32)).astype(BF)
        start_reduce(t, FR0, part.at[t, 0, 0], fin.at[t, 0, 0], x_right)
        arrived(t, QL)
        part[t, 2, 1] = (part[t, 2, 1].astype(F32) + relay[t, 1].astype(F32)).astype(BF)
        start_reduce(t, FL1, part.at[t, 2, 1], fin.at[t, 1, 1], x_left)

    def finish(t):
        for i in (FR0, FR1, FL0, FL1):
            arrived(t, i)
        far = 1 - yl
        ysend[t] = (own[t, far] + fin[t, 0, far].astype(F32) + fin[t, 1, far].astype(F32)).astype(BF)
        start_reduce(t, YL, ysend.at[t], yrecv.at[t], y_near)
        own[t, yl] = own[t, yl] + fin[t, 0, yl].astype(F32) + fin[t, 1, yl].astype(F32)

    def put(t):
        s, m = divmod(t, PARTS)
        here = slice(m * slice_rows, (m + 1) * slice_rows)
        arrived(t, YL)
        turned_product = (own[t, yl] + yrecv[t].astype(F32)).T
        off[s * W : (s + 1) * W, here] = (-turned_product).astype(BF)
        high = turned_product.astype(BF)
        low = (turned_product - high.astype(F32)).astype(BF)
        right = masked[s, here, :]
        term = jnp.dot(high, right, preferred_element_type=F32) + jnp.dot(
            low, right, preferred_element_type=F32
        )
        if m == 0:
            dacc[s] = term
        else:
            dacc[s] += term

    start_turn(0)
    start_turn(1)
    pass_hub(0)
    event0(0)
    event1(0)
    pass_hub(1)
    event2(0)
    event3(0)
    event0(1)
    event4(0)
    event1(1)
    a_copy.wait()
    dinv_copy.wait()
    event5(0)
    multiply(0)
    event2(1)
    multiply(1)
    pass_on(0)
    event3(1)
    multiply(2)
    pass_on(1)
    finish(0)
    event4(1)
    pass_on(2)
    finish(1)
    put(0)
    event5(1)
    multiply(3)
    finish(2)
    put(1)
    multiply(4)
    pass_on(3)
    put(2)
    multiply(5)
    pass_on(4)
    finish(3)
    pass_on(5)
    finish(4)
    put(3)
    finish(5)
    put(4)
    put(5)

    for s in range(SLOTS):
        dsend[s * 8 : (s + 1) * 8] = dacc[s].T.reshape(8, 16, W)

    def scatter_copy(o):
        to = (row + o) % 16
        return remote(dsend.at[to], drecv.at[o], d_send, d_recv, o, (to, col))

    def spread_copy(o):
        to = (row + o) % 16
        return remote(dsum, dall.at[row], d_send, d_recv, 16 + o, (to, col))

    @pl.loop(1, 16)
    def _(o):
        scatter_copy(o).start()

    @pl.loop(1, 16)
    def _(o):
        scatter_copy(o).wait_recv()

    total = dsend[row] + dinv[row]
    for o in range(1, 16):
        total = total + drecv[o]
    dsum[...] = total

    @pl.loop(1, 16)
    def _(o):
        spread_copy(o).start()

    diag[row] = total

    @pl.loop(1, 16)
    def _(o):
        spread_copy(o).wait_recv()
        since = (row + 16 - o) % 16
        diag[since] = dall[since]

    @pl.loop(1, 16)
    def _(o):
        scatter_copy(o).wait_send()
        spread_copy(o).wait_send()

    for c in pending:
        c.wait_send()
    for s in range(SLOTS):
        @pl.when(moves_near)
        def _():
            near_copies(s)[0].wait_send()
    end_hub()


def per_device(inverse_tiles, factor, block_mask, diag_inverse):
    rows, depth = inverse_tiles.shape
    cols = factor.shape[1]
    part_rows = rows // PARTS
    vmem = pl.BlockSpec(memory_space=pltpu.VMEM)
    anywhere = pl.BlockSpec(memory_space=pl.ANY)
    off, diag = pl.pallas_call(
        kernel,
        out_shape=(
            jax.ShapeDtypeStruct((cols, rows), BF),
            jax.ShapeDtypeStruct((16, 16, W), F32),
        ),
        in_specs=[vmem, anywhere, pl.BlockSpec(memory_space=pltpu.SMEM), anywhere],
        out_specs=(vmem, vmem),
        scratch_shapes=[
            pltpu.VMEM((rows, depth), BF),
            pltpu.VMEM((16, 16, W), F32),
            pltpu.VMEM((SLOTS, rows, W), BF),
            pltpu.VMEM((SLOTS, 2, 8, rows, W), BF),
            pltpu.VMEM((SLOTS, 2, 4, rows // 2, W), BF),
            pltpu.VMEM((SLOTS, rows, W), BF),
            pltpu.VMEM((STEPS, 3, 2, part_rows, W), BF),
            pltpu.VMEM((STEPS, 2, part_rows, W), F32),
            pltpu.VMEM((STEPS, 2, part_rows, W), BF),
            pltpu.VMEM((STEPS, 2, 2, part_rows, W), BF),
            pltpu.VMEM((STEPS, part_rows, W), BF),
            pltpu.VMEM((STEPS, part_rows, W), BF),
            pltpu.VMEM((SLOTS, W, W), F32),
            pltpu.VMEM((16, 16, W), F32),
            pltpu.VMEM((16, 16, W), F32),
            pltpu.VMEM((16, W), F32),
            pltpu.VMEM((16, 16, W), F32),
            pltpu.SemaphoreType.DMA((2,)),
            pltpu.SemaphoreType.DMA((SLOTS * GATHER,)),
            pltpu.SemaphoreType.DMA((SLOTS * GATHER,)),
            pltpu.SemaphoreType.DMA((SLOTS * 2,)),
            pltpu.SemaphoreType.DMA((SLOTS * 8,)),
            pltpu.SemaphoreType.DMA((SLOTS * 8,)),
            pltpu.SemaphoreType.DMA((SLOTS * 2,)),
            pltpu.SemaphoreType.DMA((STEPS * REDUCE,)),
            pltpu.SemaphoreType.DMA((STEPS * REDUCE,)),
            pltpu.SemaphoreType.DMA((32,)),
            pltpu.SemaphoreType.DMA((32,)),
        ],
        compiler_params=pltpu.CompilerParams(
            collective_id=0, has_side_effects=True, vmem_limit_bytes=58 * 1024 * 1024
        ),
    )(factor, inverse_tiles, block_mask, diag_inverse.reshape(8 * 16, 16, W))
    return off, diag.reshape(2, W, W)


def solution(mesh):
    return jax.shard_map(
        per_device,
        mesh=mesh,
        in_specs=(P("row", "col"), P("row", "col"), P(), P()),
        out_specs=(P("col", "row"), P("col", None, None)),
        check_vma=False,
    )
```

```python
import jax
import jax.numpy as jnp
from jax import lax
from jax.experimental import pallas as pl
from jax.experimental.pallas import tpu as pltpu
from jax.sharding import PartitionSpec as P

MESH = pl.DeviceIdType.MESH
BF = jnp.bfloat16
F32 = jnp.float32
W = 128
HALVES = 2
SLOTS = 4
PARTS = 3
STEPS = SLOTS * PARTS

Y, ZR, ZL = 0, 2, 4
RR, RL = 6, 7
SIB = 8
GATHER = 16
QR, QL, FR0, FR1, FL0, FL1, YL = range(7)
REDUCE = 7


def kernel(
    fac, a_hbm, mask, dinv_hbm, off, diag,
    a, dinv, masked, x, hub, turned, part, own, relay, fin, ysend, yrecv, dacc, dsend, drecv, dsum, dall,
    local_sem, g_send, g_recv, y_send, h_send, h_recv, f_send, t_recv, r_send, r_recv, d_send, d_recv,
):
    rows = fac.shape[0]
    slice_rows = rows // PARTS
    row, col = lax.axis_index("row"), lax.axis_index("col")
    z, yh, p = row // 4, (row // 2) % 2, row % 2
    xi, yl = col // 2, col % 2
    zr, zl, z2 = (z + 1) % 4, (z + 3) % 4, (z + 2) % 4
    xr, xl, x2 = (xi + 1) % 4, (xi + 3) % 4, (xi + 2) % 4

    def dev(z_, yh_, p_, x_, yl_):
        return (z_ * 4 + yh_ * 2 + p_, x_ * 2 + yl_)

    on_diagonal = xi == z
    moves_near = yl != yh
    y_other = dev(z, yl, p, xi, yh)
    z_right, z_left = dev(zr, yh, p, xi, yl), dev(zl, yh, p, xi, yl)
    sibling = dev(z, yh, 1 - p, xi, yl)
    x_right, x_left = dev(z, yh, p, xr, yl), dev(z, yh, p, xl, yl)
    y_near = dev(z, yh, p, xi, 1 - yl)

    dacc[...] = jnp.zeros_like(dacc)
    a_copy = pltpu.make_async_copy(a_hbm, a, local_sem.at[0])
    a_copy.start()
    dinv_copy = pltpu.make_async_copy(dinv_hbm.at[pl.ds(col * 16, 16)], dinv, local_sem.at[1])
    dinv_copy.start()

    barrier = pltpu.get_barrier_semaphore()

    @pl.loop(1, 16)
    def _(o):
        pl.semaphore_signal(barrier, inc=1, device_id=((row + o) % 16, col), device_id_type=MESH)

    for d in (x_right, x_left, dev(z, yh, p, x2, yl), y_near):
        pl.semaphore_signal(barrier, inc=1, device_id=d, device_id_type=MESH)

    @pl.when(moves_near)
    def _():
        pl.semaphore_signal(barrier, inc=1, device_id=y_other, device_id_type=MESH)

    for s in range(HALVES):
        for b in range(rows // W):
            keep = mask[row * (rows // W) + b, col * HALVES + s].astype(F32)
            block = fac[b * W : (b + 1) * W, s * W : (s + 1) * W].astype(F32)
            masked[s, b * W : (b + 1) * W, :] = (block * keep).astype(BF)

    pl.semaphore_wait(barrier, jnp.where(moves_near, 20, 19))

    pending = []

    def remote(src, dst, send, recv, i, device):
        return pltpu.make_async_remote_copy(
            src_ref=src, dst_ref=dst, send_sem=send.at[i], recv_sem=recv.at[i],
            device_id=device, device_id_type=MESH,
        )

    halves = (slice(0, rows // 2), slice(rows // 2, rows))
    quarters = [[slice((r * 2 + h) * rows // 4, (r * 2 + h + 1) * rows // 4) for h in range(2)] for r in range(2)]

    gcopies = {}

    def start_gather(u, i, src, device, r):
        ref = x.at[u, p, src, halves[r]]
        c = remote(ref, ref, g_send, g_recv, u * GATHER + i, device)
        c.start()
        gcopies[u, i] = c
        pending.append(c)

    def got(u, i):
        gcopies[u, i].wait_recv()

    def to_hub(q, h):
        s, r = divmod(q, 2)
        j = (xi - z + 4) % 4 if h == 0 else (z - xi + 4) % 4
        device = dev(z, yh, p, z, yl) if h == 0 else dev(xi, yh, p, xi, yl)
        i = (q * 2 + h) * 4
        return pltpu.make_async_remote_copy(
            src_ref=masked.at[s, quarters[r][h]], dst_ref=hub.at[q, h, j],
            send_sem=h_send.at[q * 2 + h], recv_sem=h_recv.at[i + j],
            device_id=device, device_id_type=MESH,
        )

    def from_hub(q, h, j):
        s, r = divmod(q, 2)
        device = dev((z + j) % 4, yh, p, xi, yl) if h == 0 else dev(z, yh, p, (xi + j) % 4, yl)
        i = (q * 2 + h) * 4
        return pltpu.make_async_remote_copy(
            src_ref=hub.at[q, h, j], dst_ref=turned.at[s, quarters[r][h]],
            send_sem=f_send.at[i + j], recv_sem=t_recv.at[q * 2 + h],
            device_id=device, device_id_type=MESH,
        )

    def at_hub(q, h, j):
        s, r = divmod(q, 2)
        i = (q * 2 + h) * 4
        return pltpu.make_async_copy(masked.at[s, quarters[r][h]], hub.at[q, h, j], h_recv.at[i + j])

    def stay(q, h):
        s, r = divmod(q, 2)
        rows_of = quarters[r][h]
        return pltpu.make_async_copy(masked.at[s, rows_of], turned.at[s, rows_of], t_recv.at[q * 2 + h])

    def start_turn(q):
        for h in range(2):
            @pl.when(jnp.logical_not(on_diagonal))
            def _():
                to_hub(q, h).start()

            @pl.when(on_diagonal)
            def _():
                stay(q, h).start()

    def pass_hub(q):
        @pl.when(on_diagonal)
        def _():
            for j in (1, 3, 2):
                for h in range(2):
                    at_hub(q, h, j).wait()
                    from_hub(q, h, j).start()

        @pl.when(jnp.logical_not(on_diagonal))
        def _():
            for h in range(2):
                to_hub(q, h).wait_send()

    def end_hub():
        @pl.when(on_diagonal)
        def _():
            for q in range(4):
                for h in range(2):
                    for j in (1, 3, 2):
                        from_hub(q, h, j).wait_send()

    def near_copies(u, c, r):
        src, dst = turned.at[u // 2, halves[r]], x.at[u, p, z, halves[r]]
        recv = g_recv.at[u * GATHER + Y + r]
        away = pltpu.make_async_remote_copy(
            src_ref=src, dst_ref=dst, send_sem=y_send.at[(u * 2 + c) * 2 + r], recv_sem=recv,
            device_id=dev(z, c, p, xi, yh), device_id_type=MESH,
        )
        stays = jnp.logical_and(yh == c, yl == yh)
        return away, lambda: pltpu.make_async_copy(src, dst, recv), stays

    def end_near():
        for u in range(SLOTS):
            for c in range(2):
                for r in range(2):
                    @pl.when(yl == u % 2)
                    def _():
                        away, here, stays = near_copies(u, c, r)

                        @pl.when(jnp.logical_not(stays))
                        def _():
                            away.wait_send()

    def spread_near(q):
        s, r = divmod(q, 2)
        for h in range(2):
            stay(q, h).wait()
        for e in range(2):
            for c in range(2):
                @pl.when(yl == e)
                def _():
                    away, here, stays = near_copies(s * 2 + e, c, r)

                    @pl.when(jnp.logical_not(stays))
                    def _():
                        away.start()

                    @pl.when(stays)
                    def _():
                        here().start()

    def event1(u, r):
        near_copies(u, 0, r)[1]().wait()
        start_gather(u, ZR + r, z, z_right, r)
        start_gather(u, ZL + r, z, z_left, r)
        start_gather(u, SIB + r, z, sibling, r)

    def event2(u, r):
        if r == 0:
            got(u, ZR)
            start_gather(u, RR, zl, z_right, 0)
            start_gather(u, SIB + 2, zl, sibling, 0)
        else:
            got(u, ZL + 1)
            start_gather(u, RL, zr, z_left, 1)
            start_gather(u, SIB + 3, zr, sibling, 1)

    def event3(u):
        got(u, ZL)
        start_gather(u, SIB + 4, zr, sibling, 0)
        got(u, ZR + 1)
        start_gather(u, SIB + 5, zl, sibling, 1)
        got(u, RR)
        start_gather(u, SIB + 6, z2, sibling, 0)
        got(u, RL)
        start_gather(u, SIB + 7, z2, sibling, 1)

    def event4(u):
        for i in range(8):
            got(u, SIB + i)

    def product(t, first, second):
        u, m = divmod(t, PARTS)
        here = slice(m * slice_rows, (m + 1) * slice_rows)
        total = None
        for half in range(2):
            right = jnp.concatenate([x[u, half, first], x[u, half, second]], axis=1)
            term = jnp.dot(a[here, half * rows : (half + 1) * rows], right, preferred_element_type=F32)
            total = term if total is None else total + term
        return total

    rcopies = {}

    def start_reduce(t, i, src, dst, device):
        c = remote(src, dst, r_send, r_recv, t * REDUCE + i, device)
        c.start()
        rcopies[t, i] = c
        pending.append(c)

    def arrived(t, i):
        rcopies[t, i].wait_recv()

    top, low = slice(0, slice_rows // 2), slice(slice_rows // 2, slice_rows)

    def multiply(t):
        block = product(t, xr, x2)
        part[t, 0] = block[:, :W].astype(BF)
        part[t, 1] = block[:, W:].astype(BF)
        start_reduce(t, QR, part.at[t, 1, top], relay.at[t, 0], x_right)
        start_reduce(t, QL, part.at[t, 1, low], relay.at[t, 1], x_left)
        start_reduce(t, FR1, part.at[t, 0, low], fin.at[t, 0, low], x_right)
        block = product(t, xl, xi)
        part[t, 2] = block[:, :W].astype(BF)
        start_reduce(t, FL0, part.at[t, 2, top], fin.at[t, 1, top], x_left)
        own[t] = block[:, W:]

    def pass_on(t):
        arrived(t, QR)
        part[t, 0, top] = (part[t, 0, top].astype(F32) + relay[t, 0].astype(F32)).astype(BF)
        start_reduce(t, FR0, part.at[t, 0, top], fin.at[t, 0, top], x_right)
        arrived(t, QL)
        part[t, 2, low] = (part[t, 2, low].astype(F32) + relay[t, 1].astype(F32)).astype(BF)
        start_reduce(t, FL1, part.at[t, 2, low], fin.at[t, 1, low], x_left)

    def cross(t):
        return remote(ysend.at[t], yrecv.at[t], r_send, r_recv, t * REDUCE + YL, y_near)

    def finish(t):
        e = (t // PARTS) % 2
        for i in (FR0, FR1, FL0, FL1):
            arrived(t, i)

        @pl.when(yl == e)
        def _():
            own[t] = own[t] + fin[t, 0].astype(F32) + fin[t, 1].astype(F32)

        @pl.when(yl != e)
        def _():
            ysend[t] = (own[t] + fin[t, 0].astype(F32) + fin[t, 1].astype(F32)).astype(BF)
            cross(t).start()

    def put(t):
        u, m = divmod(t, PARTS)
        s, e = divmod(u, 2)
        here = slice(m * slice_rows, (m + 1) * slice_rows)

        @pl.when(yl == e)
        def _():
            cross(t).wait_recv()
            result = (own[t] + yrecv[t].astype(F32)).T
            off[s * W : (s + 1) * W, here] = (-result).astype(BF)
            high = result.astype(BF)
            rest = (result - high.astype(F32)).astype(BF)
            right = masked[s, here, :]
            term = jnp.dot(high, right, preferred_element_type=F32) + jnp.dot(
                rest, right, preferred_element_type=F32
            )
            dacc[s] += term

    start_turn(0)
    start_turn(1)
    pass_hub(0)
    start_turn(2)
    spread_near(0)
    pass_hub(1)
    spread_near(1)
    event1(1, 0)
    event1(0, 0)
    event1(0, 1)
    a_copy.wait()
    dinv_copy.wait()
    pass_hub(2)
    event2(0, 0)
    event1(1, 1)
    spread_near(2)
    start_turn(3)
    pass_hub(3)
    event2(0, 1)
    spread_near(3)
    event1(2, 0)
    event2(1, 0)
    event2(1, 1)
    event3(0)
    event4(0)
    multiply(2)
    event1(2, 1)
    multiply(1)
    event3(1)
    event2(2, 0)
    multiply(0)
    pass_on(2)
    event4(1)
    event2(2, 1)
    pass_on(1)
    multiply(3)
    event1(3, 1)
    multiply(5)
    event1(3, 0)
    finish(1)
    event3(2)
    pass_on(0)
    multiply(4)
    finish(2)
    pass_on(3)
    event4(2)
    multiply(6)
    event2(3, 0)
    event2(3, 1)
    finish(0)
    multiply(8)
    pass_on(5)
    finish(3)
    multiply(7)
    event3(3)
    pass_on(4)
    pass_on(6)
    event4(3)
    multiply(9)
    put(1)
    put(2)
    multiply(11)
    finish(6)
    finish(4)
    pass_on(9)
    finish(5)
    pass_on(7)
    multiply(10)
    put(3)
    put(6)
    pass_on(11)
    finish(7)
    finish(9)
    pass_on(8)
    put(4)
    pass_on(10)
    finish(11)
    put(5)
    finish(8)
    finish(10)
    put(0)
    put(9)
    put(7)
    put(11)
    put(8)
    put(10)

    for s in range(HALVES):
        dsend[s * 8 : (s + 1) * 8] = dacc[s].T.reshape(8, 16, W)

    def scatter_copy(o):
        to = (row + o) % 16
        return remote(dsend.at[to], drecv.at[o], d_send, d_recv, o, (to, col))

    def spread_copy(o):
        to = (row + o) % 16
        return remote(dsum, dall.at[row], d_send, d_recv, 16 + o, (to, col))

    @pl.loop(1, 16)
    def _(o):
        scatter_copy(o).start()

    @pl.loop(1, 16)
    def _(o):
        scatter_copy(o).wait_recv()

    total = dsend[row] + dinv[row]
    for o in range(1, 16):
        total = total + drecv[o]
    dsum[...] = total

    @pl.loop(1, 16)
    def _(o):
        spread_copy(o).start()

    diag[row] = total

    @pl.loop(1, 16)
    def _(o):
        spread_copy(o).wait_recv()
        since = (row + 16 - o) % 16
        diag[since] = dall[since]

    @pl.loop(1, 16)
    def _(o):
        scatter_copy(o).wait_send()
        spread_copy(o).wait_send()

    for c in pending:
        c.wait_send()
    end_near()
    for t in range(STEPS):
        @pl.when(yl != (t // PARTS) % 2)
        def _():
            cross(t).wait_send()

    end_hub()


def per_device(inverse_tiles, factor, block_mask, diag_inverse):
    rows, depth = inverse_tiles.shape
    cols = factor.shape[1]
    part_rows = rows // PARTS
    vmem = pl.BlockSpec(memory_space=pltpu.VMEM)
    anywhere = pl.BlockSpec(memory_space=pl.ANY)
    off, diag = pl.pallas_call(
        kernel,
        out_shape=(
            jax.ShapeDtypeStruct((cols, rows), BF),
            jax.ShapeDtypeStruct((16, 16, W), F32),
        ),
        in_specs=[vmem, anywhere, pl.BlockSpec(memory_space=pltpu.SMEM), anywhere],
        out_specs=(vmem, vmem),
        scratch_shapes=[
            pltpu.VMEM((rows, depth), BF),
            pltpu.VMEM((16, 16, W), F32),
            pltpu.VMEM((HALVES, rows, W), BF),
            pltpu.VMEM((SLOTS, 2, 4, rows, W), BF),
            pltpu.VMEM((HALVES * 2, 2, 4, rows // 4, W), BF),
            pltpu.VMEM((HALVES, rows, W), BF),
            pltpu.VMEM((STEPS, 3, part_rows, W), BF),
            pltpu.VMEM((STEPS, part_rows, W), F32),
            pltpu.VMEM((STEPS, 2, part_rows // 2, W), BF),
            pltpu.VMEM((STEPS, 2, part_rows, W), BF),
            pltpu.VMEM((STEPS, part_rows, W), BF),
            pltpu.VMEM((STEPS, part_rows, W), BF),
            pltpu.VMEM((HALVES, W, W), F32),
            pltpu.VMEM((16, 16, W), F32),
            pltpu.VMEM((16, 16, W), F32),
            pltpu.VMEM((16, W), F32),
            pltpu.VMEM((16, 16, W), F32),
            pltpu.SemaphoreType.DMA((2,)),
            pltpu.SemaphoreType.DMA((SLOTS * GATHER,)),
            pltpu.SemaphoreType.DMA((SLOTS * GATHER,)),
            pltpu.SemaphoreType.DMA((SLOTS * 4,)),
            pltpu.SemaphoreType.DMA((8,)),
            pltpu.SemaphoreType.DMA((32,)),
            pltpu.SemaphoreType.DMA((32,)),
            pltpu.SemaphoreType.DMA((8,)),
            pltpu.SemaphoreType.DMA((STEPS * REDUCE,)),
            pltpu.SemaphoreType.DMA((STEPS * REDUCE,)),
            pltpu.SemaphoreType.DMA((32,)),
            pltpu.SemaphoreType.DMA((32,)),
        ],
        compiler_params=pltpu.CompilerParams(
            collective_id=0, has_side_effects=True, vmem_limit_bytes=58 * 1024 * 1024
        ),
    )(factor, inverse_tiles, block_mask, diag_inverse.reshape(8 * 16, 16, W))
    return off, diag.reshape(2, W, W)


def solution(mesh):
    return jax.shard_map(
        per_device,
        mesh=mesh,
        in_specs=(P("row", "col"), P("row", "col"), P(), P()),
        out_specs=(P("col", "row"), P("col", None, None)),
        check_vma=False,
    )
```

```python
import jax
import jax.numpy as jnp
from jax import lax
from jax.experimental import pallas as pl
from jax.experimental.pallas import tpu as pltpu
from jax.sharding import PartitionSpec as P

MESH = pl.DeviceIdType.MESH
BF = jnp.bfloat16
F32 = jnp.float32
W = 128
HALVES = 2
SLOTS = 4
PARTS = 3
STEPS = SLOTS * PARTS

PIECES = (4, 2)
QUEUE = [(s, r) for s in range(HALVES) for r in range(PIECES[s])]

Y, ZR, ZL, ON = 0, 4, 8, 12
SIB = 16
GATHER = 28
QR, QL, FR0, FR1, FL0, FL1, YL = range(7)
REDUCE = 7


def kernel(
    fac, a_hbm, mask, dinv_hbm, off, diag,
    a, dinv, masked, x, hub, turned, part, own, relay, fin, ysend, yrecv, dacc, dsend, drecv, dsum, dall,
    local_sem, g_send, g_recv, y_send, h_send, h_recv, f_send, t_recv, r_send, r_recv, d_send, d_recv,
):
    rows = fac.shape[0]
    slice_rows = rows // PARTS
    row, col = lax.axis_index("row"), lax.axis_index("col")
    z, yh, p = row // 4, (row // 2) % 2, row % 2
    xi, yl = col // 2, col % 2
    zr, zl, z2 = (z + 1) % 4, (z + 3) % 4, (z + 2) % 4
    xr, xl, x2 = (xi + 1) % 4, (xi + 3) % 4, (xi + 2) % 4

    def dev(z_, yh_, p_, x_, yl_):
        return (z_ * 4 + yh_ * 2 + p_, x_ * 2 + yl_)

    on_diagonal = xi == z
    moves_near = yl != yh
    y_other = dev(z, yl, p, xi, yh)
    z_right, z_left = dev(zr, yh, p, xi, yl), dev(zl, yh, p, xi, yl)
    sibling = dev(z, yh, 1 - p, xi, yl)
    x_right, x_left = dev(z, yh, p, xr, yl), dev(z, yh, p, xl, yl)
    y_near = dev(z, yh, p, xi, 1 - yl)

    dacc[...] = jnp.zeros_like(dacc)
    a_copy = pltpu.make_async_copy(a_hbm, a, local_sem.at[0])
    a_copy.start()
    dinv_copy = pltpu.make_async_copy(dinv_hbm.at[pl.ds(col * 16, 16)], dinv, local_sem.at[1])
    dinv_copy.start()

    barrier = pltpu.get_barrier_semaphore()

    @pl.loop(1, 16)
    def _(o):
        pl.semaphore_signal(barrier, inc=1, device_id=((row + o) % 16, col), device_id_type=MESH)

    for d in (x_right, x_left, dev(z, yh, p, x2, yl), y_near):
        pl.semaphore_signal(barrier, inc=1, device_id=d, device_id_type=MESH)

    @pl.when(moves_near)
    def _():
        pl.semaphore_signal(barrier, inc=1, device_id=y_other, device_id_type=MESH)

    for s in range(HALVES):
        for b in range(rows // W):
            keep = mask[row * (rows // W) + b, col * HALVES + s].astype(F32)
            block = fac[b * W : (b + 1) * W, s * W : (s + 1) * W].astype(F32)
            masked[s, b * W : (b + 1) * W, :] = (block * keep).astype(BF)

    pl.semaphore_wait(barrier, jnp.where(moves_near, 20, 19))

    pending = []

    def remote(src, dst, send, recv, i, device):
        return pltpu.make_async_remote_copy(
            src_ref=src, dst_ref=dst, send_sem=send.at[i], recv_sem=recv.at[i],
            device_id=device, device_id_type=MESH,
        )

    halves = (slice(0, rows // 2), slice(rows // 2, rows))

    def piece(s, r):
        size = rows // PIECES[s]
        return slice(r * size, (r + 1) * size)

    def piece_half(s, r, h):
        size = rows // PIECES[s] // 2
        return slice((r * 2 + h) * size, (r * 2 + h + 1) * size)

    def in_hub(s, r):
        size = rows // PIECES[s] // 2
        return slice(r * size, (r + 1) * size)

    gcopies = {}

    def start_gather(u, i, src, device, lines):
        ref = x.at[u, p, src, lines]
        c = remote(ref, ref, g_send, g_recv, u * GATHER + i, device)
        c.start()
        gcopies[u, i] = c
        pending.append(c)

    def got(u, i):
        gcopies[u, i].wait_recv()

    def to_hub(q, h):
        s, r = QUEUE[q]
        j = (xi - z + 4) % 4 if h == 0 else (z - xi + 4) % 4
        device = dev(z, yh, p, z, yl) if h == 0 else dev(xi, yh, p, xi, yl)
        i = (q * 2 + h) * 4
        return pltpu.make_async_remote_copy(
            src_ref=masked.at[s, piece_half(s, r, h)], dst_ref=hub.at[s, h, j, in_hub(s, r)],
            send_sem=h_send.at[q * 2 + h], recv_sem=h_recv.at[i + j],
            device_id=device, device_id_type=MESH,
        )

    def from_hub(q, h, j):
        s, r = QUEUE[q]
        device = dev((z + j) % 4, yh, p, xi, yl) if h == 0 else dev(z, yh, p, (xi + j) % 4, yl)
        i = (q * 2 + h) * 4
        return pltpu.make_async_remote_copy(
            src_ref=hub.at[s, h, j, in_hub(s, r)], dst_ref=turned.at[s, piece_half(s, r, h)],
            send_sem=f_send.at[i + j], recv_sem=t_recv.at[q * 2 + h],
            device_id=device, device_id_type=MESH,
        )

    def at_hub(q, h, j):
        s, r = QUEUE[q]
        i = (q * 2 + h) * 4
        return pltpu.make_async_copy(masked.at[s, piece_half(s, r, h)], hub.at[s, h, j, in_hub(s, r)], h_recv.at[i + j])

    def stay(q, h):
        s, r = QUEUE[q]
        rows_of = piece_half(s, r, h)
        return pltpu.make_async_copy(masked.at[s, rows_of], turned.at[s, rows_of], t_recv.at[q * 2 + h])

    def start_turn(q):
        for h in range(2):
            @pl.when(jnp.logical_not(on_diagonal))
            def _():
                to_hub(q, h).start()

            @pl.when(on_diagonal)
            def _():
                stay(q, h).start()

    def pass_hub(q):
        @pl.when(on_diagonal)
        def _():
            for j in (1, 3, 2):
                for h in range(2):
                    at_hub(q, h, j).wait()
                    from_hub(q, h, j).start()

        @pl.when(jnp.logical_not(on_diagonal))
        def _():
            for h in range(2):
                to_hub(q, h).wait_send()

    def end_hub():
        @pl.when(on_diagonal)
        def _():
            for q in range(len(QUEUE)):
                for h in range(2):
                    for j in (1, 3, 2):
                        from_hub(q, h, j).wait_send()

    def near_copies(u, c, r):
        lines = piece(u // 2, r)
        src, dst = turned.at[u // 2, lines], x.at[u, p, z, lines]
        recv = g_recv.at[u * GATHER + Y + r]
        away = pltpu.make_async_remote_copy(
            src_ref=src, dst_ref=dst, send_sem=y_send.at[(u * 2 + c) * 4 + r], recv_sem=recv,
            device_id=dev(z, c, p, xi, yh), device_id_type=MESH,
        )
        stays = jnp.logical_and(yh == c, yl == yh)
        return away, lambda: pltpu.make_async_copy(src, dst, recv), stays

    def end_near():
        for u in range(SLOTS):
            for c in range(2):
                for r in range(PIECES[u // 2]):
                    @pl.when(yl == u % 2)
                    def _():
                        away, here, stays = near_copies(u, c, r)

                        @pl.when(jnp.logical_not(stays))
                        def _():
                            away.wait_send()

    def spread_near(q):
        s, r = QUEUE[q]
        for h in range(2):
            stay(q, h).wait()
        for e in range(2):
            for c in range(2):
                @pl.when(yl == e)
                def _():
                    away, here, stays = near_copies(s * 2 + e, c, r)

                    @pl.when(jnp.logical_not(stays))
                    def _():
                        away.start()

                    @pl.when(stays)
                    def _():
                        here().start()

    def event1(u, r):
        near_copies(u, 0, r)[1]().wait()
        lines = piece(u // 2, r)
        start_gather(u, ZR + r, z, z_right, lines)
        start_gather(u, ZL + r, z, z_left, lines)
        start_gather(u, SIB + r, z, sibling, lines)

    def event2(u, r):
        n = PIECES[u // 2]
        lines = piece(u // 2, r)
        if r < n // 2:
            got(u, ZR + r)
            start_gather(u, ON + r, zl, z_right, lines)
            start_gather(u, SIB + n + r, zl, sibling, lines)
        else:
            got(u, ZL + r)
            start_gather(u, ON + r, zr, z_left, lines)
            start_gather(u, SIB + n + r, zr, sibling, lines)

    def event3(u):
        n = PIECES[u // 2]
        for r in range(n // 2):
            got(u, ZL + r)
        start_gather(u, SIB + 2 * n, zr, sibling, halves[0])
        for r in range(n // 2, n):
            got(u, ZR + r)
        start_gather(u, SIB + 2 * n + 1, zl, sibling, halves[1])
        for r in range(n // 2):
            got(u, ON + r)
        start_gather(u, SIB + 2 * n + 2, z2, sibling, halves[0])
        for r in range(n // 2, n):
            got(u, ON + r)
        start_gather(u, SIB + 2 * n + 3, z2, sibling, halves[1])

    def event4(u):
        for i in range(2 * PIECES[u // 2] + 4):
            got(u, SIB + i)

    def product(t, first, second):
        u, m = divmod(t, PARTS)
        here = slice(m * slice_rows, (m + 1) * slice_rows)
        total = None
        for half in range(2):
            right = jnp.concatenate([x[u, half, first], x[u, half, second]], axis=1)
            term = jnp.dot(a[here, half * rows : (half + 1) * rows], right, preferred_element_type=F32)
            total = term if total is None else total + term
        return total

    rcopies = {}

    def start_reduce(t, i, src, dst, device):
        c = remote(src, dst, r_send, r_recv, t * REDUCE + i, device)
        c.start()
        rcopies[t, i] = c
        pending.append(c)

    def arrived(t, i):
        rcopies[t, i].wait_recv()

    top, low = slice(0, slice_rows // 2), slice(slice_rows // 2, slice_rows)

    def multiply(t):
        block = product(t, xr, x2)
        part[t, 0] = block[:, :W].astype(BF)
        part[t, 1] = block[:, W:].astype(BF)
        start_reduce(t, QR, part.at[t, 1, top], relay.at[t, 0], x_right)
        start_reduce(t, QL, part.at[t, 1, low], relay.at[t, 1], x_left)
        start_reduce(t, FR1, part.at[t, 0, low], fin.at[t, 0, low], x_right)
        block = product(t, xl, xi)
        part[t, 2] = block[:, :W].astype(BF)
        start_reduce(t, FL0, part.at[t, 2, top], fin.at[t, 1, top], x_left)
        own[t] = block[:, W:]

    def pass_on(t):
        arrived(t, QR)
        part[t, 0, top] = (part[t, 0, top].astype(F32) + relay[t, 0].astype(F32)).astype(BF)
        start_reduce(t, FR0, part.at[t, 0, top], fin.at[t, 0, top], x_right)
        arrived(t, QL)
        part[t, 2, low] = (part[t, 2, low].astype(F32) + relay[t, 1].astype(F32)).astype(BF)
        start_reduce(t, FL1, part.at[t, 2, low], fin.at[t, 1, low], x_left)

    def cross(t):
        return remote(ysend.at[t], yrecv.at[t], r_send, r_recv, t * REDUCE + YL, y_near)

    def finish(t):
        e = (t // PARTS) % 2
        for i in (FR0, FR1, FL0, FL1):
            arrived(t, i)

        @pl.when(yl == e)
        def _():
            own[t] = own[t] + fin[t, 0].astype(F32) + fin[t, 1].astype(F32)

        @pl.when(yl != e)
        def _():
            ysend[t] = (own[t] + fin[t, 0].astype(F32) + fin[t, 1].astype(F32)).astype(BF)
            cross(t).start()

    def put(t):
        u, m = divmod(t, PARTS)
        s, e = divmod(u, 2)
        here = slice(m * slice_rows, (m + 1) * slice_rows)

        @pl.when(yl == e)
        def _():
            cross(t).wait_recv()
            result = (own[t] + yrecv[t].astype(F32)).T
            off[s * W : (s + 1) * W, here] = (-result).astype(BF)
            high = result.astype(BF)
            rest = (result - high.astype(F32)).astype(BF)
            right = masked[s, here, :]
            term = jnp.dot(high, right, preferred_element_type=F32) + jnp.dot(
                rest, right, preferred_element_type=F32
            )
            dacc[s] += term

    start_turn(0)
    start_turn(1)
    start_turn(2)
    pass_hub(0)
    pass_hub(1)
    pass_hub(2)
    spread_near(0)
    start_turn(3)
    a_copy.wait()
    dinv_copy.wait()
    pass_hub(3)
    spread_near(1)
    event1(1, 0)
    spread_near(2)
    event1(0, 0)
    spread_near(3)
    event1(0, 1)
    start_turn(4)
    pass_hub(4)
    start_turn(5)
    event1(0, 2)
    event1(0, 3)
    pass_hub(5)
    event2(0, 0)
    event2(0, 1)
    spread_near(4)
    event2(0, 2)
    event2(0, 3)
    spread_near(5)
    event1(1, 2)
    event1(1, 1)
    event3(0)
    event2(1, 0)
    event1(1, 3)
    event2(1, 2)
    event4(0)
    multiply(1)
    event2(1, 1)
    event2(1, 3)
    multiply(0)
    event1(2, 1)
    pass_on(1)
    event3(1)
    event1(2, 0)
    multiply(2)
    event2(2, 1)
    pass_on(0)
    event4(1)
    multiply(4)
    event2(2, 0)
    pass_on(2)
    multiply(3)
    event1(3, 0)
    multiply(5)
    finish(1)
    pass_on(4)
    event1(3, 1)
    event3(2)
    pass_on(3)
    event4(2)
    multiply(6)
    event2(3, 1)
    event2(3, 0)
    multiply(7)
    pass_on(5)
    finish(0)
    finish(3)
    multiply(8)
    pass_on(6)
    event3(3)
    finish(4)
    put(3)
    pass_on(7)
    event4(3)
    multiply(9)
    put(0)
    multiply(11)
    finish(7)
    finish(5)
    finish(6)
    pass_on(9)
    multiply(10)
    put(1)
    put(4)
    pass_on(11)
    finish(2)
    finish(9)
    pass_on(8)
    put(7)
    pass_on(10)
    finish(11)
    put(6)
    finish(8)
    finish(10)
    put(2)
    put(5)
    put(9)
    put(11)
    put(8)
    put(10)

    for s in range(HALVES):
        dsend[s * 8 : (s + 1) * 8] = dacc[s].T.reshape(8, 16, W)

    def scatter_copy(o):
        to = (row + o) % 16
        return remote(dsend.at[to], drecv.at[o], d_send, d_recv, o, (to, col))

    def spread_copy(o):
        to = (row + o) % 16
        return remote(dsum, dall.at[row], d_send, d_recv, 16 + o, (to, col))

    @pl.loop(1, 16)
    def _(o):
        scatter_copy(o).start()

    @pl.loop(1, 16)
    def _(o):
        scatter_copy(o).wait_recv()

    total = dsend[row] + dinv[row]
    for o in range(1, 16):
        total = total + drecv[o]
    dsum[...] = total

    @pl.loop(1, 16)
    def _(o):
        spread_copy(o).start()

    diag[row] = total

    @pl.loop(1, 16)
    def _(o):
        spread_copy(o).wait_recv()
        since = (row + 16 - o) % 16
        diag[since] = dall[since]

    @pl.loop(1, 16)
    def _(o):
        scatter_copy(o).wait_send()
        spread_copy(o).wait_send()

    for c in pending:
        c.wait_send()
    end_near()
    for t in range(STEPS):
        @pl.when(yl != (t // PARTS) % 2)
        def _():
            cross(t).wait_send()

    end_hub()


def per_device(inverse_tiles, factor, block_mask, diag_inverse):
    rows, depth = inverse_tiles.shape
    cols = factor.shape[1]
    part_rows = rows // PARTS
    vmem = pl.BlockSpec(memory_space=pltpu.VMEM)
    anywhere = pl.BlockSpec(memory_space=pl.ANY)
    off, diag = pl.pallas_call(
        kernel,
        out_shape=(
            jax.ShapeDtypeStruct((cols, rows), BF),
            jax.ShapeDtypeStruct((16, 16, W), F32),
        ),
        in_specs=[vmem, anywhere, pl.BlockSpec(memory_space=pltpu.SMEM), anywhere],
        out_specs=(vmem, vmem),
        scratch_shapes=[
            pltpu.VMEM((rows, depth), BF),
            pltpu.VMEM((16, 16, W), F32),
            pltpu.VMEM((HALVES, rows, W), BF),
            pltpu.VMEM((SLOTS, 2, 4, rows, W), BF),
            pltpu.VMEM((HALVES, 2, 4, rows // 2, W), BF),
            pltpu.VMEM((HALVES, rows, W), BF),
            pltpu.VMEM((STEPS, 3, part_rows, W), BF),
            pltpu.VMEM((STEPS, part_rows, W), F32),
            pltpu.VMEM((STEPS, 2, part_rows // 2, W), BF),
            pltpu.VMEM((STEPS, 2, part_rows, W), BF),
            pltpu.VMEM((STEPS, part_rows, W), BF),
            pltpu.VMEM((STEPS, part_rows, W), BF),
            pltpu.VMEM((HALVES, W, W), F32),
            pltpu.VMEM((16, 16, W), F32),
            pltpu.VMEM((16, 16, W), F32),
            pltpu.VMEM((16, W), F32),
            pltpu.VMEM((16, 16, W), F32),
            pltpu.SemaphoreType.DMA((2,)),
            pltpu.SemaphoreType.DMA((SLOTS * GATHER,)),
            pltpu.SemaphoreType.DMA((SLOTS * GATHER,)),
            pltpu.SemaphoreType.DMA((SLOTS * 8,)),
            pltpu.SemaphoreType.DMA((len(QUEUE) * 2,)),
            pltpu.SemaphoreType.DMA((len(QUEUE) * 8,)),
            pltpu.SemaphoreType.DMA((len(QUEUE) * 8,)),
            pltpu.SemaphoreType.DMA((len(QUEUE) * 2,)),
            pltpu.SemaphoreType.DMA((STEPS * REDUCE,)),
            pltpu.SemaphoreType.DMA((STEPS * REDUCE,)),
            pltpu.SemaphoreType.DMA((32,)),
            pltpu.SemaphoreType.DMA((32,)),
        ],
        compiler_params=pltpu.CompilerParams(
            collective_id=0, has_side_effects=True, vmem_limit_bytes=58 * 1024 * 1024
        ),
    )(factor, inverse_tiles, block_mask, diag_inverse.reshape(8 * 16, 16, W))
    return off, diag.reshape(2, W, W)


def solution(mesh):
    return jax.shard_map(
        per_device,
        mesh=mesh,
        in_specs=(P("row", "col"), P("row", "col"), P(), P()),
        out_specs=(P("col", "row"), P("col", None, None)),
        check_vma=False,
    )
```

```python
import jax
import jax.numpy as jnp
from jax import lax
from jax.experimental import pallas as pl
from jax.experimental.pallas import tpu as pltpu
from jax.sharding import PartitionSpec as P

MESH = pl.DeviceIdType.MESH
BF = jnp.bfloat16
F32 = jnp.float32
W = 128
HALVES = 2
SLOTS = 4
PARTS = 3
SHARES = ((4, 4, 4), (4, 4, 4), (4, 4, 4), (5, 5, 2))
STEPS = SLOTS * PARTS

PIECES = (4, 2)
QUEUE = [(s, r) for s in range(HALVES) for r in range(PIECES[s])]

Y, ZR, ZL, ON = 0, 4, 8, 12
SIB = 16
SENDS = 24
ARRIVALS = (0, 28, 56, 72)
QR, QL, FR0, FR1, FL0, FL1 = range(6)
REDUCE = 6
TURNS = 6


def kernel(
    fac, a_hbm, mask, dinv_hbm, off, diag,
    a, dinv, masked, x, hub, turned, part, own, relay, fin, ysend, yrecv, dacc, dsend, drecv, dsum, dall,
    local_sem, g_send, g_recv, y_send, h_recv, f_send, t_recv, r_send, r_recv, c_send, c_recv, d_send, d_recv,
):
    rows = fac.shape[0]
    unit = rows // 12

    def step_rows(t):
        u, m = divmod(t, PARTS)
        first = sum(SHARES[u][:m])
        return slice(first * unit, (first + SHARES[u][m]) * unit)

    def step_size(t):
        u, m = divmod(t, PARTS)
        return SHARES[u][m] * unit

    row, col = lax.axis_index("row"), lax.axis_index("col")
    z, yh, p = row // 4, (row // 2) % 2, row % 2
    xi, yl = col // 2, col % 2
    zr, zl, z2 = (z + 1) % 4, (z + 3) % 4, (z + 2) % 4
    xr, xl, x2 = (xi + 1) % 4, (xi + 3) % 4, (xi + 2) % 4

    def dev(z_, yh_, p_, x_, yl_):
        return (z_ * 4 + yh_ * 2 + p_, x_ * 2 + yl_)

    on_diagonal = xi == z
    moves_near = yl != yh
    y_other = dev(z, yl, p, xi, yh)
    z_right, z_left = dev(zr, yh, p, xi, yl), dev(zl, yh, p, xi, yl)
    sibling = dev(z, yh, 1 - p, xi, yl)
    x_right, x_left = dev(z, yh, p, xr, yl), dev(z, yh, p, xl, yl)
    y_near = dev(z, yh, p, xi, 1 - yl)

    dacc[...] = jnp.zeros_like(dacc)
    a_copy = pltpu.make_async_copy(a_hbm, a, local_sem.at[0])
    a_copy.start()
    dinv_copy = pltpu.make_async_copy(dinv_hbm.at[pl.ds(col * 16, 16)], dinv, local_sem.at[1])
    dinv_copy.start()

    barrier = pltpu.get_barrier_semaphore()

    @pl.loop(1, 16)
    def _(o):
        pl.semaphore_signal(barrier, inc=1, device_id=((row + o) % 16, col), device_id_type=MESH)

    for d in (x_right, x_left, dev(z, yh, p, x2, yl), y_near):
        pl.semaphore_signal(barrier, inc=1, device_id=d, device_id_type=MESH)

    @pl.when(moves_near)
    def _():
        pl.semaphore_signal(barrier, inc=1, device_id=y_other, device_id_type=MESH)

    for s in range(HALVES):
        for b in range(rows // W):
            keep = mask[row * (rows // W) + b, col * HALVES + s].astype(F32)
            block = fac[b * W : (b + 1) * W, s * W : (s + 1) * W].astype(F32)
            masked[s, b * W : (b + 1) * W, :] = (block * keep).astype(BF)

    pl.semaphore_wait(barrier, jnp.where(moves_near, 20, 19))

    active = {}

    def remote(src, dst, send, recv, device):
        return pltpu.make_async_remote_copy(
            src_ref=src, dst_ref=dst, send_sem=send, recv_sem=recv, device_id=device, device_id_type=MESH,
        )

    def start(copy, kind, i):
        if (kind, i) in active:
            active[kind, i].wait_send()
        copy.start()
        active[kind, i] = copy

    halves = (slice(0, rows // 2), slice(rows // 2, rows))

    def piece(s, r):
        size = rows // PIECES[s]
        return slice(r * size, (r + 1) * size)

    def piece_half(s, r, h):
        size = rows // PIECES[s] // 2
        return slice((r * 2 + h) * size, (r * 2 + h + 1) * size)

    def in_hub(s, r):
        size = rows // PIECES[s] // 2
        return slice(r * size, (r + 1) * size)

    gcopies = {}

    def start_gather(u, i, src, device, lines):
        n = PIECES[u // 2]
        i_here = 3 * n + i - SIB if i >= SIB else (i // 4 - 1) * n + i % 4
        ref = x.at[u, p, src, lines]
        i_send = u % 2 * SENDS + i_here
        c = remote(ref, ref, g_send.at[i_send], g_recv.at[ARRIVALS[u] + n + i_here], device)
        start(c, "gather", i_send)
        gcopies[u, i] = c

    def got(u, i):
        gcopies[u, i].wait_recv()

    def to_hub(q, h):
        s, r = QUEUE[q]
        j = (xi - z + 4) % 4 if h == 0 else (z - xi + 4) % 4
        device = dev(z, yh, p, z, yl) if h == 0 else dev(xi, yh, p, xi, yl)
        i = (q * 2 + h) * 3 - 1
        return pltpu.make_async_remote_copy(
            src_ref=masked.at[s, piece_half(s, r, h)], dst_ref=hub.at[s, h, j, in_hub(s, r)],
            send_sem=f_send.at[i + 1], recv_sem=h_recv.at[i + j],
            device_id=device, device_id_type=MESH,
        )

    def from_hub(q, h, j):
        s, r = QUEUE[q]
        device = dev((z + j) % 4, yh, p, xi, yl) if h == 0 else dev(z, yh, p, (xi + j) % 4, yl)
        i = (q * 2 + h) * 3 - 1
        return pltpu.make_async_remote_copy(
            src_ref=hub.at[s, h, j, in_hub(s, r)], dst_ref=turned.at[s, piece_half(s, r, h)],
            send_sem=f_send.at[i + j], recv_sem=t_recv.at[q * 2 + h],
            device_id=device, device_id_type=MESH,
        )

    def at_hub(q, h, j):
        s, r = QUEUE[q]
        i = (q * 2 + h) * 3 - 1
        return pltpu.make_async_copy(masked.at[s, piece_half(s, r, h)], hub.at[s, h, j, in_hub(s, r)], h_recv.at[i + j])

    def stay(q, h):
        s, r = QUEUE[q]
        rows_of = piece_half(s, r, h)
        return pltpu.make_async_copy(masked.at[s, rows_of], turned.at[s, rows_of], t_recv.at[q * 2 + h])

    def start_turn(q):
        for h in range(2):
            @pl.when(jnp.logical_not(on_diagonal))
            def _():
                to_hub(q, h).start()

            @pl.when(on_diagonal)
            def _():
                stay(q, h).start()

    def pass_hub(q):
        @pl.when(on_diagonal)
        def _():
            for j in (1, 3, 2):
                for h in range(2):
                    at_hub(q, h, j).wait()
                    from_hub(q, h, j).start()

        @pl.when(jnp.logical_not(on_diagonal))
        def _():
            for h in range(2):
                to_hub(q, h).wait_send()

    def end_hub():
        @pl.when(on_diagonal)
        def _():
            for q in range(len(QUEUE)):
                for h in range(2):
                    for j in (1, 3, 2):
                        from_hub(q, h, j).wait_send()

    def near_copies(u, c, r):
        lines = piece(u // 2, r)
        src, dst = turned.at[u // 2, lines], x.at[u, p, z, lines]
        recv = g_recv.at[ARRIVALS[u] + r]
        away = pltpu.make_async_remote_copy(
            src_ref=src, dst_ref=dst, send_sem=y_send.at[u // 2 * 8 + c * PIECES[u // 2] + r], recv_sem=recv,
            device_id=dev(z, c, p, xi, yh), device_id_type=MESH,
        )
        stays = jnp.logical_and(yh == c, yl == yh)
        return away, lambda: pltpu.make_async_copy(src, dst, recv), stays

    def end_near():
        for u in range(SLOTS):
            for c in range(2):
                for r in range(PIECES[u // 2]):
                    @pl.when(yl == u % 2)
                    def _():
                        away, here, stays = near_copies(u, c, r)

                        @pl.when(jnp.logical_not(stays))
                        def _():
                            away.wait_send()

    def spread_near(q):
        s, r = QUEUE[q]
        for h in range(2):
            stay(q, h).wait()
        for e in range(2):
            for c in range(2):
                @pl.when(yl == e)
                def _():
                    away, here, stays = near_copies(s * 2 + e, c, r)

                    @pl.when(jnp.logical_not(stays))
                    def _():
                        away.start()

                    @pl.when(stays)
                    def _():
                        here().start()

    def event1(u, r):
        near_copies(u, 0, r)[1]().wait()
        lines = piece(u // 2, r)
        start_gather(u, ZR + r, z, z_right, lines)
        start_gather(u, ZL + r, z, z_left, lines)
        start_gather(u, SIB + r, z, sibling, lines)

    def event2(u, r):
        n = PIECES[u // 2]
        lines = piece(u // 2, r)
        if r < n // 2:
            got(u, ZR + r)
            start_gather(u, ON + r, zl, z_right, lines)
            start_gather(u, SIB + n + r, zl, sibling, lines)
        else:
            got(u, ZL + r)
            start_gather(u, ON + r, zr, z_left, lines)
            start_gather(u, SIB + n + r, zr, sibling, lines)

    def event3(u):
        n = PIECES[u // 2]
        for r in range(n // 2):
            got(u, ZL + r)
        start_gather(u, SIB + 2 * n, zr, sibling, halves[0])
        for r in range(n // 2, n):
            got(u, ZR + r)
        start_gather(u, SIB + 2 * n + 1, zl, sibling, halves[1])
        for r in range(n // 2):
            got(u, ON + r)
        start_gather(u, SIB + 2 * n + 2, z2, sibling, halves[0])
        for r in range(n // 2, n):
            got(u, ON + r)
        start_gather(u, SIB + 2 * n + 3, z2, sibling, halves[1])

    def event4(u):
        for i in range(2 * PIECES[u // 2] + 4):
            got(u, SIB + i)

    def product(t, first, second):
        u, m = divmod(t, PARTS)
        here = step_rows(t)
        total = None
        for half in range(2):
            right = jnp.concatenate([x[u, half, first], x[u, half, second]], axis=1)
            term = jnp.dot(a[here, half * rows : (half + 1) * rows], right, preferred_element_type=F32)
            total = term if total is None else total + term
        return total

    rcopies = {}

    def start_reduce(t, i, src, dst, device):
        i_send = t % TURNS * REDUCE + i
        c = remote(src, dst, r_send.at[i_send], r_recv.at[t * REDUCE + i], device)
        start(c, "reduce", i_send)
        rcopies[t, i] = c

    def arrived(t, i):
        rcopies[t, i].wait_recv()

    def multiply(t):
        n = step_size(t)
        top, low, full = slice(0, n // 2), slice(n // 2, n), slice(0, n)
        block = product(t, xr, x2)
        part[t, 0, full] = block[:, :W].astype(BF)
        part[t, 1, full] = block[:, W:].astype(BF)
        start_reduce(t, QR, part.at[t, 1, top], relay.at[t, 0, top], x_right)
        start_reduce(t, QL, part.at[t, 1, low], relay.at[t, 1, top], x_left)
        start_reduce(t, FR1, part.at[t, 0, low], fin.at[t, 0, low], x_right)
        block = product(t, xl, xi)
        part[t, 2, full] = block[:, :W].astype(BF)
        start_reduce(t, FL0, part.at[t, 2, top], fin.at[t, 1, top], x_left)
        own[t, full] = block[:, W:]

    def pass_on(t):
        n = step_size(t)
        top, low = slice(0, n // 2), slice(n // 2, n)
        arrived(t, QR)
        part[t, 0, top] = (part[t, 0, top].astype(F32) + relay[t, 0, top].astype(F32)).astype(BF)
        start_reduce(t, FR0, part.at[t, 0, top], fin.at[t, 0, top], x_right)
        arrived(t, QL)
        part[t, 2, low] = (part[t, 2, low].astype(F32) + relay[t, 1, top].astype(F32)).astype(BF)
        start_reduce(t, FL1, part.at[t, 2, low], fin.at[t, 1, low], x_left)

    def cross(t):
        full = slice(0, step_size(t))
        i = t // 6 * 3 + t % 3
        return remote(ysend.at[t, full], yrecv.at[t, full], c_send.at[i], c_recv.at[i], y_near)

    def finish(t):
        e = (t // PARTS) % 2
        full = slice(0, step_size(t))
        for i in (FR0, FR1, FL0, FL1):
            arrived(t, i)

        @pl.when(yl == e)
        def _():
            own[t, full] = own[t, full] + fin[t, 0, full].astype(F32) + fin[t, 1, full].astype(F32)

        @pl.when(yl != e)
        def _():
            total = own[t, full] + fin[t, 0, full].astype(F32) + fin[t, 1, full].astype(F32)
            ysend[t, full] = total.astype(BF)
            cross(t).start()

    def put(t):
        u, m = divmod(t, PARTS)
        s, e = divmod(u, 2)
        here, full = step_rows(t), slice(0, step_size(t))

        @pl.when(yl == e)
        def _():
            cross(t).wait_recv()
            result = (own[t, full] + yrecv[t, full].astype(F32)).T
            off[s * W : (s + 1) * W, here] = (-result).astype(BF)
            high = result.astype(BF)
            rest = (result - high.astype(F32)).astype(BF)
            right = masked[s, here, :]
            term = jnp.dot(high, right, preferred_element_type=F32) + jnp.dot(
                rest, right, preferred_element_type=F32
            )
            dacc[s] += term

    start_turn(0)
    start_turn(1)
    start_turn(2)
    pass_hub(0)
    pass_hub(1)
    pass_hub(2)
    spread_near(0)
    start_turn(3)
    a_copy.wait()
    dinv_copy.wait()
    pass_hub(3)
    spread_near(1)
    event1(1, 0)
    spread_near(2)
    event1(0, 0)
    spread_near(3)
    event1(0, 1)
    start_turn(4)
    pass_hub(4)
    start_turn(5)
    event1(0, 2)
    event1(0, 3)
    pass_hub(5)
    event2(0, 0)
    event2(0, 1)
    spread_near(4)
    event2(0, 2)
    event2(0, 3)
    spread_near(5)
    event1(1, 2)
    event1(1, 1)
    event3(0)
    event2(1, 0)
    event1(1, 3)
    event2(1, 2)
    event4(0)
    multiply(1)
    event2(1, 1)
    event2(1, 3)
    multiply(0)
    event1(2, 1)
    pass_on(1)
    event3(1)
    event1(2, 0)
    multiply(2)
    event2(2, 1)
    pass_on(0)
    event4(1)
    multiply(4)
    event2(2, 0)
    pass_on(2)
    multiply(3)
    event1(3, 0)
    multiply(5)
    finish(1)
    pass_on(4)
    event1(3, 1)
    event3(2)
    pass_on(3)
    event4(2)
    multiply(6)
    event2(3, 1)
    event2(3, 0)
    multiply(7)
    pass_on(5)
    finish(0)
    finish(3)
    multiply(8)
    pass_on(6)
    event3(3)
    finish(4)
    put(3)
    pass_on(7)
    event4(3)
    multiply(9)
    put(0)
    multiply(11)
    finish(7)
    finish(5)
    finish(6)
    pass_on(9)
    multiply(10)
    put(1)
    put(4)
    pass_on(11)
    finish(2)
    finish(9)
    pass_on(8)
    put(7)
    pass_on(10)
    finish(11)
    put(6)
    finish(8)
    finish(10)
    put(2)
    put(5)
    put(9)
    put(11)
    put(8)
    put(10)

    for s in range(HALVES):
        dsend[s * 8 : (s + 1) * 8] = dacc[s].T.reshape(8, 16, W)

    def scatter_copy(o):
        to = (row + o) % 16
        return remote(dsend.at[to], drecv.at[o], d_send.at[o - 1], d_recv.at[o - 1], (to, col))

    def spread_copy(o):
        to = (row + o) % 16
        return remote(dsum, dall.at[row], d_send.at[o - 1], d_recv.at[o + 14], (to, col))

    @pl.loop(1, 16)
    def _(o):
        scatter_copy(o).start()

    for c in active.values():
        c.wait_send()
    end_near()
    for t in range(STEPS):
        @pl.when(yl != (t // PARTS) % 2)
        def _():
            cross(t).wait_send()

    end_hub()

    @pl.loop(1, 16)
    def _(o):
        scatter_copy(o).wait()

    total = dsend[row] + dinv[row]
    for o in range(1, 16):
        total = total + drecv[o]
    dsum[...] = total

    @pl.loop(1, 16)
    def _(o):
        spread_copy(o).start()

    diag[row] = total

    @pl.loop(1, 16)
    def _(o):
        spread_copy(o).wait_recv()
        since = (row + 16 - o) % 16
        diag[since] = dall[since]

    @pl.loop(1, 16)
    def _(o):
        spread_copy(o).wait_send()


def per_device(inverse_tiles, factor, block_mask, diag_inverse):
    rows, depth = inverse_tiles.shape
    cols = factor.shape[1]
    part_rows = rows // 12 * max(max(shares) for shares in SHARES)
    vmem = pl.BlockSpec(memory_space=pltpu.VMEM)
    anywhere = pl.BlockSpec(memory_space=pl.ANY)
    off, diag = pl.pallas_call(
        kernel,
        out_shape=(
            jax.ShapeDtypeStruct((cols, rows), BF),
            jax.ShapeDtypeStruct((16, 16, W), F32),
        ),
        in_specs=[vmem, anywhere, pl.BlockSpec(memory_space=pltpu.SMEM), anywhere],
        out_specs=(vmem, vmem),
        scratch_shapes=[
            pltpu.VMEM((rows, depth), BF),
            pltpu.VMEM((16, 16, W), F32),
            pltpu.VMEM((HALVES, rows, W), BF),
            pltpu.VMEM((SLOTS, 2, 4, rows, W), BF),
            pltpu.VMEM((HALVES, 2, 4, rows // 2, W), BF),
            pltpu.VMEM((HALVES, rows, W), BF),
            pltpu.VMEM((STEPS, 3, part_rows, W), BF),
            pltpu.VMEM((STEPS, part_rows, W), F32),
            pltpu.VMEM((STEPS, 2, part_rows // 2, W), BF),
            pltpu.VMEM((STEPS, 2, part_rows, W), BF),
            pltpu.VMEM((STEPS, part_rows, W), BF),
            pltpu.VMEM((STEPS, part_rows, W), BF),
            pltpu.VMEM((HALVES, W, W), F32),
            pltpu.VMEM((16, 16, W), F32),
            pltpu.VMEM((16, 16, W), F32),
            pltpu.VMEM((16, W), F32),
            pltpu.VMEM((16, 16, W), F32),
            pltpu.SemaphoreType.DMA((2,)),
            pltpu.SemaphoreType.DMA((2 * SENDS,)),
            pltpu.SemaphoreType.DMA((88,)),
            pltpu.SemaphoreType.DMA((12,)),
            pltpu.SemaphoreType.DMA((len(QUEUE) * 6,)),
            pltpu.SemaphoreType.DMA((len(QUEUE) * 6,)),
            pltpu.SemaphoreType.DMA((len(QUEUE) * 2,)),
            pltpu.SemaphoreType.DMA((TURNS * REDUCE,)),
            pltpu.SemaphoreType.DMA((STEPS * REDUCE,)),
            pltpu.SemaphoreType.DMA((6,)),
            pltpu.SemaphoreType.DMA((6,)),
            pltpu.SemaphoreType.DMA((15,)),
            pltpu.SemaphoreType.DMA((30,)),
        ],
        compiler_params=pltpu.CompilerParams(
            collective_id=0, has_side_effects=True, vmem_limit_bytes=58 * 1024 * 1024
        ),
    )(factor, inverse_tiles, block_mask, diag_inverse.reshape(8 * 16, 16, W))
    return off, diag.reshape(2, W, W)


def solution(mesh):
    return jax.shard_map(
        per_device,
        mesh=mesh,
        in_specs=(P("row", "col"), P("row", "col"), P(), P()),
        out_specs=(P("col", "row"), P("col", None, None)),
        check_vma=False,
    )
```

```python
import jax
import jax.numpy as jnp
from jax import lax
from jax.experimental import pallas as pl
from jax.experimental.pallas import tpu as pltpu
from jax.sharding import PartitionSpec as P

MESH = pl.DeviceIdType.MESH
BF = jnp.bfloat16
F32 = jnp.float32
W = 128
HALVES = 2
SLOTS = 4
PARTS = 3
SHARES = ((5, 2, 5), (4, 4, 4), (4, 4, 4), (5, 5, 2))
STEPS = SLOTS * PARTS

PIECES = (4, 2)
QUEUE = [(s, r) for s in range(HALVES) for r in range(PIECES[s])]

Y, ZR, ZL, ON = 0, 4, 8, 12
SIB = 16
SENDS = 24
ARRIVALS = (0, 28, 56, 72)
QR, QL, FR0, FR1, FL0, FL1 = range(6)
REDUCE = 6
TURNS = 6


def kernel(
    fac, a_hbm, mask, dinv_hbm, off, diag,
    a, dinv, masked, x, hub, turned, part, own, relay, fin, ysend, yrecv, dacc, dsend, drecv, dsum, dall,
    local_sem, g_send, g_recv, y_send, h_recv, f_send, t_recv, r_send, r_recv, c_send, c_recv, d_send, d_recv,
):
    rows = fac.shape[0]
    unit = rows // 12

    def step_rows(t):
        u, m = divmod(t, PARTS)
        first = sum(SHARES[u][:m])
        return slice(first * unit, (first + SHARES[u][m]) * unit)

    def step_size(t):
        u, m = divmod(t, PARTS)
        return SHARES[u][m] * unit

    row, col = lax.axis_index("row"), lax.axis_index("col")
    z, yh, p = row // 4, (row // 2) % 2, row % 2
    xi, yl = col // 2, col % 2
    zr, zl, z2 = (z + 1) % 4, (z + 3) % 4, (z + 2) % 4
    xr, xl, x2 = (xi + 1) % 4, (xi + 3) % 4, (xi + 2) % 4

    def dev(z_, yh_, p_, x_, yl_):
        return (z_ * 4 + yh_ * 2 + p_, x_ * 2 + yl_)

    on_diagonal = xi == z
    moves_near = yl != yh
    y_other = dev(z, yl, p, xi, yh)
    z_right, z_left = dev(zr, yh, p, xi, yl), dev(zl, yh, p, xi, yl)
    sibling = dev(z, yh, 1 - p, xi, yl)
    x_right, x_left = dev(z, yh, p, xr, yl), dev(z, yh, p, xl, yl)
    y_near = dev(z, yh, p, xi, 1 - yl)

    dacc[...] = jnp.zeros_like(dacc)
    a_copy = pltpu.make_async_copy(a_hbm, a, local_sem.at[0])
    a_copy.start()
    dinv_copy = pltpu.make_async_copy(dinv_hbm.at[pl.ds(col * 16, 16)], dinv, local_sem.at[1])
    dinv_copy.start()

    barrier = pltpu.get_barrier_semaphore()

    @pl.loop(1, 16)
    def _(o):
        pl.semaphore_signal(barrier, inc=1, device_id=((row + o) % 16, col), device_id_type=MESH)

    for d in (x_right, x_left, dev(z, yh, p, x2, yl), y_near):
        pl.semaphore_signal(barrier, inc=1, device_id=d, device_id_type=MESH)

    @pl.when(moves_near)
    def _():
        pl.semaphore_signal(barrier, inc=1, device_id=y_other, device_id_type=MESH)

    for s in range(HALVES):
        for b in range(rows // W):
            keep = mask[row * (rows // W) + b, col * HALVES + s].astype(F32)
            block = fac[b * W : (b + 1) * W, s * W : (s + 1) * W].astype(F32)
            masked[s, b * W : (b + 1) * W, :] = (block * keep).astype(BF)

    pl.semaphore_wait(barrier, jnp.where(moves_near, 20, 19))

    active = {}

    def remote(src, dst, send, recv, device):
        return pltpu.make_async_remote_copy(
            src_ref=src, dst_ref=dst, send_sem=send, recv_sem=recv, device_id=device, device_id_type=MESH,
        )

    def start(copy, kind, i):
        if (kind, i) in active:
            active[kind, i].wait_send()
        copy.start()
        active[kind, i] = copy

    halves = (slice(0, rows // 2), slice(rows // 2, rows))

    def piece(s, r):
        size = rows // PIECES[s]
        return slice(r * size, (r + 1) * size)

    def piece_half(s, r, h):
        size = rows // PIECES[s] // 2
        return slice((r * 2 + h) * size, (r * 2 + h + 1) * size)

    def in_hub(s, r):
        size = rows // PIECES[s] // 2
        return slice(r * size, (r + 1) * size)

    gcopies = {}

    def start_gather(u, i, src, device, lines):
        n = PIECES[u // 2]
        i_here = 3 * n + i - SIB if i >= SIB else (i // 4 - 1) * n + i % 4
        ref = x.at[u, p, src, lines]
        i_send = u % 2 * SENDS + i_here
        c = remote(ref, ref, g_send.at[i_send], g_recv.at[ARRIVALS[u] + n + i_here], device)
        start(c, "gather", i_send)
        gcopies[u, i] = c

    def got(u, i):
        gcopies[u, i].wait_recv()

    def to_hub(q, h):
        s, r = QUEUE[q]
        j = (xi - z + 4) % 4 if h == 0 else (z - xi + 4) % 4
        device = dev(z, yh, p, z, yl) if h == 0 else dev(xi, yh, p, xi, yl)
        i = (q * 2 + h) * 3 - 1
        return pltpu.make_async_remote_copy(
            src_ref=masked.at[s, piece_half(s, r, h)], dst_ref=hub.at[s, h, j, in_hub(s, r)],
            send_sem=f_send.at[i + 1], recv_sem=h_recv.at[i + j],
            device_id=device, device_id_type=MESH,
        )

    def from_hub(q, h, j):
        s, r = QUEUE[q]
        device = dev((z + j) % 4, yh, p, xi, yl) if h == 0 else dev(z, yh, p, (xi + j) % 4, yl)
        i = (q * 2 + h) * 3 - 1
        return pltpu.make_async_remote_copy(
            src_ref=hub.at[s, h, j, in_hub(s, r)], dst_ref=turned.at[s, piece_half(s, r, h)],
            send_sem=f_send.at[i + j], recv_sem=t_recv.at[q * 2 + h],
            device_id=device, device_id_type=MESH,
        )

    def at_hub(q, h, j):
        s, r = QUEUE[q]
        i = (q * 2 + h) * 3 - 1
        return pltpu.make_async_copy(masked.at[s, piece_half(s, r, h)], hub.at[s, h, j, in_hub(s, r)], h_recv.at[i + j])

    def stay(q, h):
        s, r = QUEUE[q]
        rows_of = piece_half(s, r, h)
        return pltpu.make_async_copy(masked.at[s, rows_of], turned.at[s, rows_of], t_recv.at[q * 2 + h])

    def start_turn(q):
        for h in range(2):
            @pl.when(jnp.logical_not(on_diagonal))
            def _():
                to_hub(q, h).start()

            @pl.when(on_diagonal)
            def _():
                stay(q, h).start()

    def pass_hub(q):
        @pl.when(on_diagonal)
        def _():
            for j in (1, 3, 2):
                for h in range(2):
                    at_hub(q, h, j).wait()
                    from_hub(q, h, j).start()

        @pl.when(jnp.logical_not(on_diagonal))
        def _():
            for h in range(2):
                to_hub(q, h).wait_send()

    def end_hub():
        @pl.when(on_diagonal)
        def _():
            for q in range(len(QUEUE)):
                for h in range(2):
                    for j in (1, 3, 2):
                        from_hub(q, h, j).wait_send()

    def near_copies(u, c, r):
        lines = piece(u // 2, r)
        src, dst = turned.at[u // 2, lines], x.at[u, p, z, lines]
        recv = g_recv.at[ARRIVALS[u] + r]
        away = pltpu.make_async_remote_copy(
            src_ref=src, dst_ref=dst, send_sem=y_send.at[u // 2 * 8 + c * PIECES[u // 2] + r], recv_sem=recv,
            device_id=dev(z, c, p, xi, yh), device_id_type=MESH,
        )
        stays = jnp.logical_and(yh == c, yl == yh)
        return away, lambda: pltpu.make_async_copy(src, dst, recv), stays

    def end_near():
        for u in range(SLOTS):
            for c in range(2):
                for r in range(PIECES[u // 2]):
                    @pl.when(yl == u % 2)
                    def _():
                        away, here, stays = near_copies(u, c, r)

                        @pl.when(jnp.logical_not(stays))
                        def _():
                            away.wait_send()

    def spread_near(q):
        s, r = QUEUE[q]
        for h in range(2):
            stay(q, h).wait()
        for e in range(2):
            for c in range(2):
                @pl.when(yl == e)
                def _():
                    away, here, stays = near_copies(s * 2 + e, c, r)

                    @pl.when(jnp.logical_not(stays))
                    def _():
                        away.start()

                    @pl.when(stays)
                    def _():
                        here().start()

    def event1(u, r):
        near_copies(u, 0, r)[1]().wait()
        lines = piece(u // 2, r)
        start_gather(u, ZR + r, z, z_right, lines)
        start_gather(u, ZL + r, z, z_left, lines)
        start_gather(u, SIB + r, z, sibling, lines)

    def event2(u, r):
        n = PIECES[u // 2]
        lines = piece(u // 2, r)
        if r < n // 2:
            got(u, ZR + r)
            start_gather(u, ON + r, zl, z_right, lines)
            start_gather(u, SIB + n + r, zl, sibling, lines)
        else:
            got(u, ZL + r)
            start_gather(u, ON + r, zr, z_left, lines)
            start_gather(u, SIB + n + r, zr, sibling, lines)

    def event3(u):
        n = PIECES[u // 2]
        for r in range(n // 2):
            got(u, ZL + r)
        start_gather(u, SIB + 2 * n, zr, sibling, halves[0])
        for r in range(n // 2, n):
            got(u, ZR + r)
        start_gather(u, SIB + 2 * n + 1, zl, sibling, halves[1])
        for r in range(n // 2):
            got(u, ON + r)
        start_gather(u, SIB + 2 * n + 2, z2, sibling, halves[0])
        for r in range(n // 2, n):
            got(u, ON + r)
        start_gather(u, SIB + 2 * n + 3, z2, sibling, halves[1])

    def event4(u):
        for i in range(2 * PIECES[u // 2] + 4):
            got(u, SIB + i)

    def product(t, first, second):
        u, m = divmod(t, PARTS)
        here = step_rows(t)
        total = None
        for half in range(2):
            right = jnp.concatenate([x[u, half, first], x[u, half, second]], axis=1)
            term = jnp.dot(a[here, half * rows : (half + 1) * rows], right, preferred_element_type=F32)
            total = term if total is None else total + term
        return total

    rcopies = {}

    def start_reduce(t, i, src, dst, device):
        i_send = t % TURNS * REDUCE + i
        c = remote(src, dst, r_send.at[i_send], r_recv.at[t * REDUCE + i], device)
        start(c, "reduce", i_send)
        rcopies[t, i] = c

    def arrived(t, i):
        rcopies[t, i].wait_recv()

    def multiply(t):
        n = step_size(t)
        top, low, full = slice(0, n // 2), slice(n // 2, n), slice(0, n)
        block = product(t, xr, x2)
        part[t, 0, full] = block[:, :W].astype(BF)
        part[t, 1, full] = block[:, W:].astype(BF)
        start_reduce(t, QR, part.at[t, 1, top], relay.at[t, 0, top], x_right)
        start_reduce(t, QL, part.at[t, 1, low], relay.at[t, 1, top], x_left)
        start_reduce(t, FR1, part.at[t, 0, low], fin.at[t, 0, low], x_right)
        block = product(t, xl, xi)
        part[t, 2, full] = block[:, :W].astype(BF)
        start_reduce(t, FL0, part.at[t, 2, top], fin.at[t, 1, top], x_left)
        own[t, full] = block[:, W:]

    def pass_on(t):
        n = step_size(t)
        top, low = slice(0, n // 2), slice(n // 2, n)
        arrived(t, QR)
        part[t, 0, top] = (part[t, 0, top].astype(F32) + relay[t, 0, top].astype(F32)).astype(BF)
        start_reduce(t, FR0, part.at[t, 0, top], fin.at[t, 0, top], x_right)
        arrived(t, QL)
        part[t, 2, low] = (part[t, 2, low].astype(F32) + relay[t, 1, top].astype(F32)).astype(BF)
        start_reduce(t, FL1, part.at[t, 2, low], fin.at[t, 1, low], x_left)

    def cross(t):
        full = slice(0, step_size(t))
        i = t // 6 * 3 + t % 3
        return remote(ysend.at[t, full], yrecv.at[t, full], c_send.at[i], c_recv.at[i], y_near)

    def finish(t):
        e = (t // PARTS) % 2
        full = slice(0, step_size(t))
        for i in (FR0, FR1, FL0, FL1):
            arrived(t, i)

        @pl.when(yl == e)
        def _():
            own[t, full] = own[t, full] + fin[t, 0, full].astype(F32) + fin[t, 1, full].astype(F32)

        @pl.when(yl != e)
        def _():
            total = own[t, full] + fin[t, 0, full].astype(F32) + fin[t, 1, full].astype(F32)
            ysend[t, full] = total.astype(BF)
            cross(t).start()

    def put(t):
        u, m = divmod(t, PARTS)
        s, e = divmod(u, 2)
        here, full = step_rows(t), slice(0, step_size(t))

        @pl.when(yl == e)
        def _():
            cross(t).wait_recv()
            result = (own[t, full] + yrecv[t, full].astype(F32)).T
            off[s * W : (s + 1) * W, here] = (-result).astype(BF)
            high = result.astype(BF)
            rest = (result - high.astype(F32)).astype(BF)
            right = masked[s, here, :]
            term = jnp.dot(high, right, preferred_element_type=F32) + jnp.dot(
                rest, right, preferred_element_type=F32
            )
            dacc[s] += term

    start_turn(0)
    start_turn(1)
    start_turn(2)
    pass_hub(0)
    pass_hub(1)
    pass_hub(2)
    spread_near(0)
    start_turn(3)
    a_copy.wait()
    dinv_copy.wait()
    pass_hub(3)
    spread_near(1)
    event1(1, 0)
    spread_near(2)
    event1(0, 0)
    spread_near(3)
    event1(0, 1)
    start_turn(4)
    pass_hub(4)
    start_turn(5)
    event1(0, 2)
    event1(0, 3)
    pass_hub(5)
    event2(0, 0)
    event2(0, 1)
    spread_near(4)
    event2(0, 2)
    event2(0, 3)
    spread_near(5)
    event1(1, 2)
    event1(1, 1)
    event3(0)
    event2(1, 0)
    event1(1, 3)
    event2(1, 2)
    event4(0)
    multiply(1)
    event2(1, 1)
    event2(1, 3)
    multiply(0)
    event1(2, 1)
    pass_on(1)
    event3(1)
    event1(2, 0)
    multiply(2)
    event2(2, 1)
    pass_on(0)
    event4(1)
    multiply(4)
    event2(2, 0)
    pass_on(2)
    multiply(3)
    event1(3, 0)
    multiply(5)
    finish(1)
    pass_on(4)
    event1(3, 1)
    event3(2)
    pass_on(3)
    event4(2)
    multiply(6)
    event2(3, 1)
    event2(3, 0)
    multiply(7)
    pass_on(5)
    finish(0)
    finish(3)
    multiply(8)
    pass_on(6)
    event3(3)
    finish(4)
    put(3)
    pass_on(7)
    event4(3)
    multiply(9)
    put(0)
    multiply(11)
    finish(7)
    finish(5)
    finish(6)
    pass_on(9)
    multiply(10)
    put(1)
    put(4)
    pass_on(11)
    finish(2)
    finish(9)
    pass_on(8)
    put(7)
    pass_on(10)
    finish(11)
    put(6)
    finish(8)
    finish(10)
    put(2)
    put(5)
    put(9)
    put(11)
    put(8)
    put(10)

    for s in range(HALVES):
        dsend[s * 8 : (s + 1) * 8] = dacc[s].T.reshape(8, 16, W)

    def scatter_copy(o):
        to = (row + o) % 16
        return remote(dsend.at[to], drecv.at[o], d_send.at[o - 1], d_recv.at[o - 1], (to, col))

    def spread_copy(o):
        to = (row + o) % 16
        return remote(dsum, dall.at[row], d_send.at[o - 1], d_recv.at[o + 14], (to, col))

    @pl.loop(1, 16)
    def _(o):
        scatter_copy(o).start()

    for c in active.values():
        c.wait_send()
    end_near()
    for t in range(STEPS):
        @pl.when(yl != (t // PARTS) % 2)
        def _():
            cross(t).wait_send()

    end_hub()

    @pl.loop(1, 16)
    def _(o):
        scatter_copy(o).wait()

    total = dsend[row] + dinv[row]
    for o in range(1, 16):
        total = total + drecv[o]
    dsum[...] = total

    @pl.loop(1, 16)
    def _(o):
        spread_copy(o).start()

    diag[row] = total

    @pl.loop(1, 16)
    def _(o):
        spread_copy(o).wait_recv()
        since = (row + 16 - o) % 16
        diag[since] = dall[since]

    @pl.loop(1, 16)
    def _(o):
        spread_copy(o).wait_send()


def per_device(inverse_tiles, factor, block_mask, diag_inverse):
    rows, depth = inverse_tiles.shape
    cols = factor.shape[1]
    part_rows = rows // 12 * max(max(shares) for shares in SHARES)
    vmem = pl.BlockSpec(memory_space=pltpu.VMEM)
    anywhere = pl.BlockSpec(memory_space=pl.ANY)
    off, diag = pl.pallas_call(
        kernel,
        out_shape=(
            jax.ShapeDtypeStruct((cols, rows), BF),
            jax.ShapeDtypeStruct((16, 16, W), F32),
        ),
        in_specs=[vmem, anywhere, pl.BlockSpec(memory_space=pltpu.SMEM), anywhere],
        out_specs=(vmem, vmem),
        scratch_shapes=[
            pltpu.VMEM((rows, depth), BF),
            pltpu.VMEM((16, 16, W), F32),
            pltpu.VMEM((HALVES, rows, W), BF),
            pltpu.VMEM((SLOTS, 2, 4, rows, W), BF),
            pltpu.VMEM((HALVES, 2, 4, rows // 2, W), BF),
            pltpu.VMEM((HALVES, rows, W), BF),
            pltpu.VMEM((STEPS, 3, part_rows, W), BF),
            pltpu.VMEM((STEPS, part_rows, W), F32),
            pltpu.VMEM((STEPS, 2, part_rows // 2, W), BF),
            pltpu.VMEM((STEPS, 2, part_rows, W), BF),
            pltpu.VMEM((STEPS, part_rows, W), BF),
            pltpu.VMEM((STEPS, part_rows, W), BF),
            pltpu.VMEM((HALVES, W, W), F32),
            pltpu.VMEM((16, 16, W), F32),
            pltpu.VMEM((16, 16, W), F32),
            pltpu.VMEM((16, W), F32),
            pltpu.VMEM((16, 16, W), F32),
            pltpu.SemaphoreType.DMA((2,)),
            pltpu.SemaphoreType.DMA((2 * SENDS,)),
            pltpu.SemaphoreType.DMA((88,)),
            pltpu.SemaphoreType.DMA((12,)),
            pltpu.SemaphoreType.DMA((len(QUEUE) * 6,)),
            pltpu.SemaphoreType.DMA((len(QUEUE) * 6,)),
            pltpu.SemaphoreType.DMA((len(QUEUE) * 2,)),
            pltpu.SemaphoreType.DMA((TURNS * REDUCE,)),
            pltpu.SemaphoreType.DMA((STEPS * REDUCE,)),
            pltpu.SemaphoreType.DMA((6,)),
            pltpu.SemaphoreType.DMA((6,)),
            pltpu.SemaphoreType.DMA((15,)),
            pltpu.SemaphoreType.DMA((30,)),
        ],
        compiler_params=pltpu.CompilerParams(
            collective_id=0, has_side_effects=True, vmem_limit_bytes=58 * 1024 * 1024
        ),
    )(factor, inverse_tiles, block_mask, diag_inverse.reshape(8 * 16, 16, W))
    return off, diag.reshape(2, W, W)


def solution(mesh):
    return jax.shard_map(
        per_device,
        mesh=mesh,
        in_specs=(P("row", "col"), P("row", "col"), P(), P()),
        out_specs=(P("col", "row"), P("col", None, None)),
        check_vma=False,
    )
```
